32 devices in a mesh: dp: 8 (over z, core), space: 4 (over y, x).
Axes of the slice: x: 2, y: 2, z: 4, core: 2. Of those that a mesh axis runs over, the one named last changes fastest.
Arguments:
- query: bfloat16 [8, 1536, 1536], P('dp', 'space'), may hold values from -8 to 8
- key_in: bfloat16 [8, 1536, 1536], P('dp', 'space'), may hold values from -8 to 8
- value_in: bfloat16 [8, 1536, 1536], P('dp', 'space'), may hold values from -6 to 6
- out_weight: bfloat16 [1536, 3072], P('dp'), may hold values from -0.15625 to 0.15625
- grad_out: bfloat16 [8, 1536, 3072], P('dp', 'space'), may hold values from -6 to 6
- neighbours: int32 [4, 3], replicated, may hold values from -1 to 3, as said below
Outputs:
- mixed: bfloat16 [8, 1536, 3072], P('dp', 'space')
- grad_query: bfloat16 [8, 1536, 1536], P('dp', 'space')
- grad_key: bfloat16 [8, 1536, 1536], P('dp', 'space')
- grad_value: bfloat16 [8, 1536, 1536], P('dp', 'space')
- grad_weight: float32 [1536, 3072], P('dp')
The draws below stay inside these ranges and needn't reach their ends.
Inputs may be any that keep to these rules, and one draw needn't show every extreme that they name: `neighbours`: entry 0 of row t is t; entry 1 is t - 1 or -1; entry 2 is t + 1 or -1.
All inputs are finite; a program needn't handle non-finite values.
Results may differ from the reference program's by a relative error of at most 0.034.
Values may be sent and summed in bfloat16 or wider, within the bound.
A program may use at most 192 MiB of HBM per device.

```python
import math
import jax
import jax.numpy as jnp
from jax import lax

D = 3072
HEADS = 12
HEAD = 128
TILE = 384
HD = 1536
TILES = 4
TOKENS = 1536
CLIPS = 8


def draw_query(key, part):
    key = jax.random.fold_in(key, 101)
    values = jnp.clip(jax.random.normal(key, (CLIPS, TOKENS, HD), jnp.float32), -6.0, 6.0)
    return values.astype(jnp.bfloat16)


def draw_key_in(key, part):
    key = jax.random.fold_in(key, 202)
    values = jnp.clip(jax.random.normal(key, (CLIPS, TOKENS, HD), jnp.float32), -6.0, 6.0)
    return values.astype(jnp.bfloat16)


def draw_neighbours(key, part):
    key = jax.random.fold_in(key, 303)
    tile_ids = jnp.arange(TILES, dtype=jnp.int32)
    living = jax.random.randint(key, (TILES, 2), 0, 3) > 0
    left_ids = jnp.where(living[:, 0] & (tile_ids >= 1), tile_ids - 1, -1)
    right_ids = jnp.where(living[:, 1] & (tile_ids < TILES - 1), tile_ids + 1, -1)
    return jnp.stack([tile_ids, left_ids, right_ids], axis=1).astype(jnp.int32)


def block_levels(own_key, extent, pieces, smallest, largest):
    level = 1.0
    for dim, shards_of in pieces:
        steps = jax.random.uniform(jax.random.fold_in(jax.random.fold_in(own_key, 6), dim), (shards_of,), jnp.float32, smallest / len(pieces), largest / len(pieces))
        level = level * jnp.repeat(jnp.exp(steps), extent[dim] // shards_of).reshape((-1,) + (1,) * (len(extent) - 1 - dim))
    return level


def normal_values(rng, dims, deviation, bound, shards=(), held_as=jnp.bfloat16):
    gain = block_levels(rng, dims, shards, -0.22, 0.18) if shards else 1.0
    array = jax.random.normal(rng, dims, jnp.float32) * deviation * gain
    return jnp.minimum(jnp.maximum(array, -bound), bound).astype(held_as)


def setup_inputs(seed: int = 0) -> dict:
    key_of = jax.random.split(jax.random.key(seed), 7)
    query = draw_query(jax.random.fold_in(key_of[6], 71), 0)
    key_in = draw_key_in(jax.random.fold_in(key_of[6], 71), 0)
    value_in = normal_values(key_of[2], (CLIPS, TOKENS, HD), 1.0, 6.0, ((0, 8), (1, 4)))
    out_weight = normal_values(key_of[3], (HD, D), HD ** -0.5, 0.15625, ((0, 8),))
    grad_out = normal_values(key_of[4], (CLIPS, TOKENS, D), 1.0, 6.0, ((0, 8), (1, 4)))
    neighbours = draw_neighbours(jax.random.fold_in(key_of[6], 71), 0)
    return dict(query=query, key_in=key_in, value_in=value_in, out_weight=out_weight, grad_out=grad_out, neighbours=neighbours)


masked_score = -1e+30

def tile_window(blocks, axis):
    padding = [(1, 1)] + [(0, 0)] * (blocks.ndim - 1)
    padded = jnp.pad(blocks, padding)
    return jnp.concatenate([padded[:-2], padded[1:-1], padded[2:]], axis=axis)

def rounded(values):
    return lax.optimization_barrier(values.astype(jnp.bfloat16))

def reference(query, key_in, value_in, out_weight, grad_out, neighbours):
    tile_total = TOKENS // TILE
    score_scale = 1.0 / math.sqrt(HEAD)
    tile_ids = jnp.arange(tile_total, dtype=jnp.int32)
    window_tiles = tile_ids[:, None] - 1 + jnp.arange(3, dtype=jnp.int32)[None, :]
    key_live = jnp.any((neighbours[:, None, :] == window_tiles[:, :, None]) & (neighbours[:, None, :] >= 0), axis=2)
    inside = (window_tiles >= 0) & (window_tiles < tile_total)
    their_lists = neighbours[jnp.clip(window_tiles, 0, tile_total - 1)]
    query_live = inside & jnp.any(their_lists == tile_ids[:, None, None], axis=2)
    key_mask = jnp.repeat(key_live, TILE, axis=1)
    query_mask = jnp.repeat(query_live, TILE, axis=1)
    shape_four = (tile_total, TILE, HEADS, HEAD)
    shape_wide = (tile_total, 3 * TILE, HEADS, HEAD)

    def one_clip(inputs):
        query_rows, key_rows, value_rows, upstream = inputs
        queries = query_rows.reshape(shape_four).astype(jnp.float32)
        keys_own = key_rows.reshape(shape_four).astype(jnp.float32)
        values_own = value_rows.reshape(shape_four).astype(jnp.float32)
        key_window = tile_window(key_rows.reshape(tile_total, TILE, HD), 1).reshape(shape_wide).astype(jnp.float32)
        value_window = tile_window(value_rows.reshape(tile_total, TILE, HD), 1).reshape(shape_wide).astype(jnp.float32)
        scores = jnp.einsum('tihd,tjhd->thij', queries, key_window) * score_scale
        scores = jnp.where(key_mask[:, None, None, :], scores, masked_score)
        row_max = lax.optimization_barrier(jnp.max(scores, axis=3, keepdims=True))
        log_total = (row_max + jnp.log(lax.optimization_barrier(jnp.sum(jnp.exp(scores - row_max), axis=3, keepdims=True))))[..., 0]
        weights = jnp.exp(scores - log_total[..., None])
        weights_bf = rounded(weights).astype(jnp.float32)
        attn = rounded(jnp.einsum('thij,tjhd->tihd', weights_bf, value_window).reshape(TOKENS, HD))
        mixed = jnp.dot(attn, out_weight, preferred_element_type=jnp.float32).astype(jnp.bfloat16)
        grad_attn = rounded(lax.dot_general(upstream, out_weight, (((1,), (1,)), ((), ())), preferred_element_type=jnp.float32))
        grad_heads = grad_attn.reshape(shape_four).astype(jnp.float32)
        deltas = lax.optimization_barrier(jnp.sum(grad_heads * attn.reshape(shape_four).astype(jnp.float32), axis=3)).transpose(0, 2, 1)
        dprob = jnp.einsum('tihd,tjhd->thij', grad_heads, value_window)
        dscore = rounded(weights * (dprob - deltas[..., None]) * score_scale).astype(jnp.float32)
        grad_query = jnp.einsum('thij,tjhd->tihd', dscore, key_window).reshape(TOKENS, HD).astype(jnp.bfloat16)
        query_window = tile_window(query_rows.reshape(tile_total, TILE, HD), 1).reshape(shape_wide).astype(jnp.float32)
        grad_window = tile_window(grad_attn.reshape(tile_total, TILE, HD), 1).reshape(shape_wide).astype(jnp.float32)
        log_window = tile_window(log_total, 2)
        delta_window = tile_window(deltas, 2)
        back_scores = jnp.einsum('tjhd,tihd->thji', query_window, keys_own) * score_scale
        back_weights = jnp.where(query_mask[:, None, :, None], jnp.exp(back_scores - log_window[..., None]), 0.0)
        back_bf = rounded(back_weights).astype(jnp.float32)
        grad_value = jnp.einsum('thji,tjhd->tihd', back_bf, grad_window).reshape(TOKENS, HD).astype(jnp.bfloat16)
        back_dprob = jnp.einsum('tjhd,tihd->thji', grad_window, values_own)
        back_dscore = rounded(back_weights * (back_dprob - delta_window[..., None]) * score_scale).astype(jnp.float32)
        grad_key = jnp.einsum('thji,tjhd->tihd', back_dscore, query_window).reshape(TOKENS, HD).astype(jnp.bfloat16)
        return (mixed, grad_query, grad_key, grad_value, attn)
    mixed, grad_query, grad_key, grad_value, attn_all = lax.map(one_clip, (query, key_in, value_in, grad_out))
    grad_weight = lax.dot_general(attn_all.reshape(CLIPS * TOKENS, HD), grad_out.reshape(CLIPS * TOKENS, D), (((0,), (0,)), ((), ())), preferred_element_type=jnp.float32)
    return (mixed, grad_query, grad_key, grad_value, grad_weight)
```

```python
import functools
import math

import jax
import jax.numpy as jnp
from jax import lax
from jax.experimental import pallas as pl
from jax.experimental.pallas import tpu as pltpu
from jax.sharding import PartitionSpec as P

HEAD = 128


masked_score = -1e30


def padded(x, sides, width):
    for axis, dim in sides:
        size, length = (lax.axis_size(axis), x.shape[dim])
        up = [(i, (i + 1) % size) for i in range(size - 1)]
        down = [(j, i) for i, j in up]
        last = lax.slice_in_dim(x, length - width, length, axis=dim)
        initial = lax.slice_in_dim(x, 0, width, axis=dim)
        before = lax.ppermute(last, axis, up)
        after = lax.ppermute(initial, axis, down)
        x = jnp.concatenate([before, x, after], axis=dim)
    return x


def halo_on_device(query, key_in, value_in, out_weight, grad_out, neighbours):
    query_rows = query[0]
    key_rows = key_in[0]
    value_rows = value_in[0]
    upstream = grad_out[0]
    tile_rows, model_cols = query_rows.shape
    head_count = model_cols // HEAD
    score_scale = 1.0 / math.sqrt(HEAD)
    tile_total = neighbours.shape[0]
    device_tile = lax.axis_index("space")
    window_tiles = device_tile - 1 + jnp.arange(3, dtype=jnp.int32)
    own_list = neighbours[device_tile]
    key_live = jnp.any(
        (own_list[None, :] == window_tiles[:, None]) & (own_list[None, :] >= 0), axis=1
    )
    inside = (window_tiles >= 0) & (window_tiles < tile_total)
    their_lists = neighbours[jnp.clip(window_tiles, 0, tile_total - 1)]
    query_live = inside & jnp.any(their_lists == device_tile, axis=1)
    key_mask = jnp.repeat(key_live, tile_rows)
    query_mask = jnp.repeat(query_live, tile_rows)
    key_value = jnp.stack([key_rows, value_rows])
    kv_near = padded(key_value, (("space", 1),), tile_rows)
    key_heads = kv_near[0].reshape(3 * tile_rows, head_count, HEAD)
    value_heads = kv_near[1].reshape(3 * tile_rows, head_count, HEAD)
    query_heads = query_rows.reshape(tile_rows, head_count, HEAD)
    scores = (
        jnp.einsum("ihd,jhd->hij", query_heads, key_heads, preferred_element_type=jnp.float32)
        * score_scale
    )
    scores = jnp.where(key_mask[None, None, :], scores, masked_score)
    row_max = jnp.max(scores, axis=2, keepdims=True)
    log_total = (row_max + jnp.log(jnp.sum(jnp.exp(scores - row_max), axis=2, keepdims=True)))[
        ..., 0
    ]
    weights = jnp.exp(scores - log_total[..., None])
    weights_bf = weights.astype(jnp.bfloat16)
    attn = (
        jnp.einsum("hij,jhd->ihd", weights_bf, value_heads, preferred_element_type=jnp.float32)
        .reshape(tile_rows, model_cols)
        .astype(jnp.bfloat16)
    )
    shard_piece = lax.all_gather(out_weight, "dp", axis=0, tiled=True)
    attn_cols = attn
    mixed_sum = jnp.dot(attn_cols, shard_piece, preferred_element_type=jnp.float32)
    new_cols = lax.dot_general(
        upstream, shard_piece, (((1,), (1,)), ((), ())), preferred_element_type=jnp.float32
    )
    back_cols = new_cols
    mixed_sum, back_cols = (mixed_sum, back_cols)
    mixed = mixed_sum.astype(jnp.bfloat16)
    grad_attn = back_cols.astype(jnp.bfloat16)
    grad_heads = grad_attn.reshape(tile_rows, head_count, HEAD)
    deltas = jnp.sum(
        grad_heads.astype(jnp.float32)
        * attn.reshape(tile_rows, head_count, HEAD).astype(jnp.float32),
        axis=2,
    ).T
    dprob = jnp.einsum("ihd,jhd->hij", grad_heads, value_heads, preferred_element_type=jnp.float32)
    dscore = (weights * (dprob - deltas[:, :, None]) * score_scale).astype(jnp.bfloat16)
    grad_query = (
        jnp.einsum("hij,jhd->ihd", dscore, key_heads, preferred_element_type=jnp.float32)
        .reshape(tile_rows, model_cols)
        .astype(jnp.bfloat16)
    )
    stat_pair = jnp.stack([log_total, deltas])
    stat_near = padded(stat_pair, (("space", 2),), tile_rows)
    query_grad = jnp.stack([query_rows, grad_attn])
    query_near = padded(query_grad, (("space", 1),), tile_rows)
    far_queries = query_near[0].reshape(3 * tile_rows, head_count, HEAD)
    far_grads = query_near[1].reshape(3 * tile_rows, head_count, HEAD)
    own_keys = key_rows.reshape(tile_rows, head_count, HEAD)
    own_values = value_rows.reshape(tile_rows, head_count, HEAD)
    back_scores = (
        jnp.einsum("jhd,ihd->hji", far_queries, own_keys, preferred_element_type=jnp.float32)
        * score_scale
    )
    back_weights = jnp.where(
        query_mask[None, :, None], jnp.exp(back_scores - stat_near[0][:, :, None]), 0.0
    )
    back_bf = back_weights.astype(jnp.bfloat16)
    grad_value = (
        jnp.einsum("hji,jhd->ihd", back_bf, far_grads, preferred_element_type=jnp.float32)
        .reshape(tile_rows, model_cols)
        .astype(jnp.bfloat16)
    )
    back_dprob = jnp.einsum(
        "jhd,ihd->hji", far_grads, own_values, preferred_element_type=jnp.float32
    )
    back_dscore = (back_weights * (back_dprob - stat_near[1][:, :, None]) * score_scale).astype(
        jnp.bfloat16
    )
    grad_key = (
        jnp.einsum("hji,jhd->ihd", back_dscore, far_queries, preferred_element_type=jnp.float32)
        .reshape(tile_rows, model_cols)
        .astype(jnp.bfloat16)
    )
    attn_cols = attn
    partial_rows = lax.psum_scatter(
        lax.dot_general(
            attn_cols, upstream, (((0,), (0,)), ((), ())), preferred_element_type=jnp.float32
        ),
        ("dp", "space"),
        scatter_dimension=0,
        tiled=True,
    )
    grad_weight = lax.all_gather(partial_rows, "space", axis=0, tiled=True)
    return (mixed[None], grad_query[None], grad_key[None], grad_value[None], grad_weight)


MESH = pl.DeviceIdType.MESH
SCALE = 1.0 / math.sqrt(HEAD)


def window(tile, tiles):
    return range(max(0, tile - 1), min(tiles, tile + 2))


def tile_bias(near, tile, other):
    live = near[tile, 0] == other
    for slot in range(1, near.shape[1]):
        live = jnp.logical_or(live, near[tile, slot] == other)
    return jnp.where(live, 0.0, masked_score).astype(jnp.float32)


def dot_nt(a, b):
    return lax.dot_general(a, b, (((1,), (1,)), ((), ())), preferred_element_type=jnp.float32)


def dot_tn(a, b):
    return lax.dot_general(a, b, (((0,), (0,)), ((), ())), preferred_element_type=jnp.float32)


def greet(n):
    me = lax.axis_index("space")
    barrier = pltpu.get_barrier_semaphore()
    for off in range(1, n):
        pl.semaphore_signal(
            barrier, inc=1, device_id={"space": lax.rem(me + off, n)}, device_id_type=MESH
        )
    pl.semaphore_wait(barrier, n - 1)


def send(src, dst, send_sem, recv_sem, peer):
    return pltpu.make_async_remote_copy(
        src_ref=src,
        dst_ref=dst,
        send_sem=send_sem,
        recv_sem=recv_sem,
        device_id={"space": peer},
        device_id_type=MESH,
    )


def to_heads(n, pairs, send_sem, recv_sem, own_sem):
    me = lax.axis_index("space")
    rows, width = pairs[0][0].shape[0], pairs[0][1].shape[1]
    mine = pl.ds(pl.multiple_of(me * rows, rows), rows)
    copies = []
    for off in range(1, n):
        peer = lax.rem(me + off, n)
        cols = pl.ds(pl.multiple_of(peer * width, width), width)
        for a, (src, dst) in enumerate(pairs):
            copy = send(
                src.at[:, cols], dst.at[mine], send_sem.at[a, off], recv_sem.at[a, off], peer
            )
            copy.start()
            copies.append(copy)
    cols = pl.ds(pl.multiple_of(me * width, width), width)
    for a, (src, dst) in enumerate(pairs):
        copy = pltpu.make_async_copy(src.at[:, cols], dst.at[mine], own_sem.at[a])
        copy.start()
        copies.append(copy)
    return copies


def forward_kernel(
    n, near, q, k, v, attn, qh, kh, vh, ah, log_total, send_sem, recv_sem, own_sem,
    back_send, back_recv, back_own,
):
    me = lax.axis_index("space")
    rows = q.shape[0]
    width = qh.shape[1]
    greet(n)
    for copy in to_heads(n, ((q, qh), (k, kh), (v, vh)), send_sem, recv_sem, own_sem):
        copy.wait()
    my_cols = pl.ds(pl.multiple_of(me * width, width), width)
    for t in range(n):
        here = pl.ds(t * rows, rows)
        biases = [tile_bias(near, t, u) for u in window(t, n)]

        def one_head(h, carry):
            cols = pl.ds(pl.multiple_of(h * HEAD, HEAD), HEAD)
            query = qh[here, cols]
            scores = [
                dot_nt(query, kh[pl.ds(u * rows, rows), cols]) * SCALE + bias
                for u, bias in zip(window(t, n), biases)
            ]
            top = functools.reduce(
                jnp.maximum, [jnp.max(s, axis=1, keepdims=True) for s in scores]
            )
            parts = [jnp.exp(s - top) for s in scores]
            total = sum(jnp.sum(p, axis=1, keepdims=True) for p in parts)
            mixed = sum(
                jnp.dot(
                    p.astype(jnp.bfloat16),
                    vh[pl.ds(u * rows, rows), cols],
                    preferred_element_type=jnp.float32,
                )
                for u, p in zip(window(t, n), parts)
            )
            ah[here, cols] = (mixed / total).astype(jnp.bfloat16)
            log_total[h, here, :] = top + jnp.log(total)
            return carry

        lax.fori_loop(0, width // HEAD, one_head, 0)

        @pl.when(me != t)
        def _():
            send(ah.at[here], attn.at[:, my_cols], back_send.at[t], back_recv.at[me], t).start()

        @pl.when(me == t)
        def _():
            pltpu.make_async_copy(ah.at[here], attn.at[:, my_cols], back_own).start()

    for off in range(1, n):
        peer = lax.rem(me + off, n)
        their = pl.ds(pl.multiple_of(peer * rows, rows), rows)
        their_cols = pl.ds(pl.multiple_of(peer * width, width), width)
        send(ah.at[their], attn.at[:, my_cols], back_send.at[peer], back_recv.at[me], peer).wait_send()
        send(
            ah.at[their], attn.at[:, their_cols], back_send.at[peer], back_recv.at[peer], peer
        ).wait_recv()
    mine = pl.ds(pl.multiple_of(me * rows, rows), rows)
    pltpu.make_async_copy(ah.at[mine], attn.at[:, my_cols], back_own).wait()


def backward_kernel(
    n, near, ga, qh, kh, vh, ah, log_total, dq, dk, dv, gh, dqh, dkh, dvh, dk_sum, dv_sum,
    send_sem, recv_sem, own_sem, back_send, back_recv, back_own,
):
    me = lax.axis_index("space")
    rows = ga.shape[0]
    width = qh.shape[1]
    greet(n)
    copies = to_heads(n, ((ga, gh),), send_sem, recv_sem, own_sem)
    dk_sum[...] = jnp.zeros_like(dk_sum)
    dv_sum[...] = jnp.zeros_like(dv_sum)
    for copy in copies:
        copy.wait()
    my_cols = pl.ds(pl.multiple_of(me * width, width), width)

    def give(a, src, dst, t):
        here = pl.ds(t * rows, rows)

        @pl.when(me != t)
        def _():
            send(
                src.at[here], dst.at[:, my_cols], back_send.at[a, t], back_recv.at[a, me], t
            ).start()

        @pl.when(me == t)
        def _():
            pltpu.make_async_copy(src.at[here], dst.at[:, my_cols], back_own.at[a]).start()

    def give_key(t):
        here = pl.ds(t * rows, rows)
        dkh[here, :] = dk_sum[here, :].astype(jnp.bfloat16)
        dvh[here, :] = dv_sum[here, :].astype(jnp.bfloat16)
        give(1, dkh, dk, t)
        give(2, dvh, dv, t)

    for t in range(n):
        here = pl.ds(t * rows, rows)
        biases = [tile_bias(near, t, u) for u in window(t, n)]

        def one_head(h, carry):
            cols = pl.ds(pl.multiple_of(h * HEAD, HEAD), HEAD)
            query, grad = qh[here, cols], gh[here, cols]
            level = log_total[h, here, :]
            delta = jnp.sum(
                grad.astype(jnp.float32) * ah[here, cols].astype(jnp.float32),
                axis=1,
                keepdims=True,
            )
            out = jnp.zeros((rows, HEAD), jnp.float32)
            for u, bias in zip(window(t, n), biases):
                there = pl.ds(u * rows, rows)
                key, value = kh[there, cols], vh[there, cols]
                weight = jnp.exp(dot_nt(query, key) * SCALE + bias - level)
                dscore = (weight * (dot_nt(grad, value) - delta) * SCALE).astype(jnp.bfloat16)
                out += jnp.dot(dscore, key, preferred_element_type=jnp.float32)
                dk_sum[there, cols] += dot_tn(dscore, query)
                dv_sum[there, cols] += dot_tn(weight.astype(jnp.bfloat16), grad)
            dqh[here, cols] = out.astype(jnp.bfloat16)
            return carry

        lax.fori_loop(0, width // HEAD, one_head, 0)
        give(0, dqh, dq, t)
        if t >= 1:
            give_key(t - 1)
    give_key(n - 1)
    mine = pl.ds(pl.multiple_of(me * rows, rows), rows)
    for a, (src, dst) in enumerate(((dqh, dq), (dkh, dk), (dvh, dv))):
        for off in range(1, n):
            peer = lax.rem(me + off, n)
            their = pl.ds(pl.multiple_of(peer * rows, rows), rows)
            their_cols = pl.ds(pl.multiple_of(peer * width, width), width)
            send(
                src.at[their], dst.at[:, my_cols], back_send.at[a, peer], back_recv.at[a, me], peer
            ).wait_send()
            send(
                src.at[their],
                dst.at[:, their_cols],
                back_send.at[a, peer],
                back_recv.at[a, peer],
                peer,
            ).wait_recv()
        pltpu.make_async_copy(src.at[mine], dst.at[:, my_cols], back_own.at[a]).wait()


def sems(*shape):
    return pltpu.SemaphoreType.DMA(shape)


def heads_on_device(n, query, key_in, value_in, out_weight, grad_out, neighbours):
    upstream = grad_out[0]
    rows, model_cols = query.shape[1:]
    width = model_cols // n
    heads = width // HEAD
    bf16, f32 = jnp.bfloat16, jnp.float32
    weight = lax.all_gather(out_weight, "dp", axis=0, tiled=True)
    hbm = pl.BlockSpec(memory_space=pl.ANY)
    vmem = pl.BlockSpec(memory_space=pltpu.VMEM)
    smem = pl.BlockSpec(memory_space=pltpu.SMEM)
    wide = jax.ShapeDtypeStruct((rows, model_cols), bf16)
    tall = jax.ShapeDtypeStruct((n * rows, width), bf16)
    level = jax.ShapeDtypeStruct((heads, n * rows, 1), f32)
    attn, qh, kh, vh, ah, log_total = pl.pallas_call(
        functools.partial(forward_kernel, n),
        out_shape=(wide, tall, tall, tall, tall, level),
        in_specs=[smem, hbm, hbm, hbm],
        out_specs=(hbm, vmem, vmem, vmem, vmem, vmem),
        scratch_shapes=[
            sems(3, n), sems(3, n), sems(3), sems(n), sems(n), pltpu.SemaphoreType.DMA,
        ],
        compiler_params=pltpu.CompilerParams(
            collective_id=0, has_side_effects=True, vmem_limit_bytes=50 * 2**20
        ),
        name="attend",
    )(neighbours, query[0], key_in[0], value_in[0])
    partial_weight = dot_tn(attn, upstream).astype(bf16)
    piece = lax.psum_scatter(partial_weight, ("dp", "space"), scatter_dimension=0, tiled=True)
    grad_attn = dot_nt(upstream, weight).astype(bf16)
    dq, dk, dv = pl.pallas_call(
        functools.partial(backward_kernel, n),
        out_shape=(wide, wide, wide),
        in_specs=[smem, hbm, vmem, vmem, vmem, vmem, vmem],
        out_specs=(hbm, hbm, hbm),
        scratch_shapes=[
            pltpu.VMEM(tall.shape, bf16),
            pltpu.VMEM(tall.shape, bf16),
            pltpu.VMEM(tall.shape, bf16),
            pltpu.VMEM(tall.shape, bf16),
            pltpu.VMEM(tall.shape, f32),
            pltpu.VMEM(tall.shape, f32),
            sems(1, n), sems(1, n), sems(1), sems(3, n), sems(3, n), sems(3),
        ],
        compiler_params=pltpu.CompilerParams(
            collective_id=1, has_side_effects=True, vmem_limit_bytes=50 * 2**20
        ),
        name="attend_back",
    )(neighbours, grad_attn, qh, kh, vh, ah, log_total)
    mixed = jnp.dot(attn, weight, preferred_element_type=f32).astype(bf16)
    grad_weight = lax.all_gather(piece, "space", axis=0, tiled=True).astype(f32)
    return (mixed[None], dq[None], dk[None], dv[None], grad_weight)


def solution(mesh):
    n = mesh.shape["space"]

    def on_device(query, *rest):
        if query.shape[2] % (n * HEAD) == 0:
            return heads_on_device(n, query, *rest)
        return halo_on_device(query, *rest)

    return jax.shard_map(
        on_device,
        mesh=mesh,
        in_specs=(
            P("dp", "space", None),
            P("dp", "space", None),
            P("dp", "space", None),
            P("dp", None),
            P("dp", "space", None),
            P(),
        ),
        out_specs=(
            P("dp", "space", None),
            P("dp", "space", None),
            P("dp", "space", None),
            P("dp", "space", None),
            P("dp", None),
        ),
        check_vma=False,
    )
```

```python
import functools
import math

import jax
import jax.numpy as jnp
from jax import lax
from jax.experimental import pallas as pl
from jax.experimental.pallas import tpu as pltpu
from jax.sharding import PartitionSpec as P

HEAD = 128


masked_score = -1e30


def padded(x, sides, width):
    for axis, dim in sides:
        size, length = (lax.axis_size(axis), x.shape[dim])
        up = [(i, (i + 1) % size) for i in range(size - 1)]
        down = [(j, i) for i, j in up]
        last = lax.slice_in_dim(x, length - width, length, axis=dim)
        initial = lax.slice_in_dim(x, 0, width, axis=dim)
        before = lax.ppermute(last, axis, up)
        after = lax.ppermute(initial, axis, down)
        x = jnp.concatenate([before, x, after], axis=dim)
    return x


def halo_on_device(query, key_in, value_in, out_weight, grad_out, neighbours):
    query_rows = query[0]
    key_rows = key_in[0]
    value_rows = value_in[0]
    upstream = grad_out[0]
    tile_rows, model_cols = query_rows.shape
    head_count = model_cols // HEAD
    score_scale = 1.0 / math.sqrt(HEAD)
    tile_total = neighbours.shape[0]
    device_tile = lax.axis_index("space")
    window_tiles = device_tile - 1 + jnp.arange(3, dtype=jnp.int32)
    own_list = neighbours[device_tile]
    key_live = jnp.any(
        (own_list[None, :] == window_tiles[:, None]) & (own_list[None, :] >= 0), axis=1
    )
    inside = (window_tiles >= 0) & (window_tiles < tile_total)
    their_lists = neighbours[jnp.clip(window_tiles, 0, tile_total - 1)]
    query_live = inside & jnp.any(their_lists == device_tile, axis=1)
    key_mask = jnp.repeat(key_live, tile_rows)
    query_mask = jnp.repeat(query_live, tile_rows)
    key_value = jnp.stack([key_rows, value_rows])
    kv_near = padded(key_value, (("space", 1),), tile_rows)
    key_heads = kv_near[0].reshape(3 * tile_rows, head_count, HEAD)
    value_heads = kv_near[1].reshape(3 * tile_rows, head_count, HEAD)
    query_heads = query_rows.reshape(tile_rows, head_count, HEAD)
    scores = (
        jnp.einsum("ihd,jhd->hij", query_heads, key_heads, preferred_element_type=jnp.float32)
        * score_scale
    )
    scores = jnp.where(key_mask[None, None, :], scores, masked_score)
    row_max = jnp.max(scores, axis=2, keepdims=True)
    log_total = (row_max + jnp.log(jnp.sum(jnp.exp(scores - row_max), axis=2, keepdims=True)))[
        ..., 0
    ]
    weights = jnp.exp(scores - log_total[..., None])
    weights_bf = weights.astype(jnp.bfloat16)
    attn = (
        jnp.einsum("hij,jhd->ihd", weights_bf, value_heads, preferred_element_type=jnp.float32)
        .reshape(tile_rows, model_cols)
        .astype(jnp.bfloat16)
    )
    shard_piece = lax.all_gather(out_weight, "dp", axis=0, tiled=True)
    attn_cols = attn
    mixed_sum = jnp.dot(attn_cols, shard_piece, preferred_element_type=jnp.float32)
    new_cols = lax.dot_general(
        upstream, shard_piece, (((1,), (1,)), ((), ())), preferred_element_type=jnp.float32
    )
    back_cols = new_cols
    mixed_sum, back_cols = (mixed_sum, back_cols)
    mixed = mixed_sum.astype(jnp.bfloat16)
    grad_attn = back_cols.astype(jnp.bfloat16)
    grad_heads = grad_attn.reshape(tile_rows, head_count, HEAD)
    deltas = jnp.sum(
        grad_heads.astype(jnp.float32)
        * attn.reshape(tile_rows, head_count, HEAD).astype(jnp.float32),
        axis=2,
    ).T
    dprob = jnp.einsum("ihd,jhd->hij", grad_heads, value_heads, preferred_element_type=jnp.float32)
    dscore = (weights * (dprob - deltas[:, :, None]) * score_scale).astype(jnp.bfloat16)
    grad_query = (
        jnp.einsum("hij,jhd->ihd", dscore, key_heads, preferred_element_type=jnp.float32)
        .reshape(tile_rows, model_cols)
        .astype(jnp.bfloat16)
    )
    stat_pair = jnp.stack([log_total, deltas])
    stat_near = padded(stat_pair, (("space", 2),), tile_rows)
    query_grad = jnp.stack([query_rows, grad_attn])
    query_near = padded(query_grad, (("space", 1),), tile_rows)
    far_queries = query_near[0].reshape(3 * tile_rows, head_count, HEAD)
    far_grads = query_near[1].reshape(3 * tile_rows, head_count, HEAD)
    own_keys = key_rows.reshape(tile_rows, head_count, HEAD)
    own_values = value_rows.reshape(tile_rows, head_count, HEAD)
    back_scores = (
        jnp.einsum("jhd,ihd->hji", far_queries, own_keys, preferred_element_type=jnp.float32)
        * score_scale
    )
    back_weights = jnp.where(
        query_mask[None, :, None], jnp.exp(back_scores - stat_near[0][:, :, None]), 0.0
    )
    back_bf = back_weights.astype(jnp.bfloat16)
    grad_value = (
        jnp.einsum("hji,jhd->ihd", back_bf, far_grads, preferred_element_type=jnp.float32)
        .reshape(tile_rows, model_cols)
        .astype(jnp.bfloat16)
    )
    back_dprob = jnp.einsum(
        "jhd,ihd->hji", far_grads, own_values, preferred_element_type=jnp.float32
    )
    back_dscore = (back_weights * (back_dprob - stat_near[1][:, :, None]) * score_scale).astype(
        jnp.bfloat16
    )
    grad_key = (
        jnp.einsum("hji,jhd->ihd", back_dscore, far_queries, preferred_element_type=jnp.float32)
        .reshape(tile_rows, model_cols)
        .astype(jnp.bfloat16)
    )
    attn_cols = attn
    partial_rows = lax.psum_scatter(
        lax.dot_general(
            attn_cols, upstream, (((0,), (0,)), ((), ())), preferred_element_type=jnp.float32
        ),
        ("dp", "space"),
        scatter_dimension=0,
        tiled=True,
    )
    grad_weight = lax.all_gather(partial_rows, "space", axis=0, tiled=True)
    return (mixed[None], grad_query[None], grad_key[None], grad_value[None], grad_weight)


MESH = pl.DeviceIdType.MESH
SCALE = 1.0 / math.sqrt(HEAD)


def window(tile, tiles):
    return range(max(0, tile - 1), min(tiles, tile + 2))


def tile_bias(near, tile, other):
    live = near[tile, 0] == other
    for slot in range(1, near.shape[1]):
        live = jnp.logical_or(live, near[tile, slot] == other)
    return jnp.where(live, 0.0, masked_score).astype(jnp.float32)


def dot_nt(a, b):
    return lax.dot_general(a, b, (((1,), (1,)), ((), ())), preferred_element_type=jnp.float32)


def dot_tn(a, b):
    return lax.dot_general(a, b, (((0,), (0,)), ((), ())), preferred_element_type=jnp.float32)


def place(nz):
    row = lax.axis_index("dp")
    return row // 2, row % 2, lax.axis_index("space")


def greet(peers):
    barrier = pltpu.get_barrier_semaphore()
    for row, column in peers:
        pl.semaphore_signal(
            barrier, inc=1, device_id={"dp": row, "space": column}, device_id_type=MESH
        )
    pl.semaphore_wait(barrier, len(peers))


def send_to(src, dst, send_sem, recv_sem, row, column):
    return pltpu.make_async_remote_copy(
        src_ref=src,
        dst_ref=dst,
        send_sem=send_sem,
        recv_sem=recv_sem,
        device_id={"dp": row, "space": column},
        device_id_type=MESH,
    )


def send(src, dst, send_sem, recv_sem, peer):
    return send_to(src, dst, send_sem, recv_sem, lax.axis_index("dp"), peer)


def block(index, size):
    return pl.ds(pl.multiple_of(index * size, size), size)


def to_heads(n, pairs, send_sem, recv_sem, own_sem):
    me = lax.axis_index("space")
    rows, width = pairs[0][0].shape[0], pairs[0][1].shape[1]
    mine = pl.ds(pl.multiple_of(me * rows, rows), rows)
    copies = []
    for off in range(1, n):
        peer = lax.rem(me + off, n)
        cols = pl.ds(pl.multiple_of(peer * width, width), width)
        for a, (src, dst) in enumerate(pairs):
            copy = send(
                src.at[:, cols], dst.at[mine], send_sem.at[a, off], recv_sem.at[a, off], peer
            )
            copy.start()
            copies.append(copy)
    cols = pl.ds(pl.multiple_of(me * width, width), width)
    for a, (src, dst) in enumerate(pairs):
        copy = pltpu.make_async_copy(src.at[:, cols], dst.at[mine], own_sem.at[a])
        copy.start()
        copies.append(copy)
    return copies


def forward_kernel(
    n, nz, near, q, k, v, g, w, attn, attn_other, g_other, wf, qh, kh, vh, ah, log_total,
    send_sem, recv_sem, own_sem, back_send, back_recv, back_own,
    core_send, core_recv, zq_send, zq_recv, zh_send, zh_recv, sq_send, sq_recv,
    cq_send, cq_recv, ch_send, ch_recv,
):
    z, core, me = place(nz)
    mine_dp = 2 * z + core
    twin = 2 * z + 1 - core
    rows = q.shape[0]
    width = qh.shape[1]
    depth, model = w.shape
    half = model // 2
    quarter = half // n
    upper = pl.ds(half, half)
    greet(
        [(mine_dp, lax.rem(me + o, n)) for o in range(1, n)]
        + [(2 * lax.rem(z + o, nz) + core, me) for o in range(1, nz)]
        + [(twin, me)]
    )
    shard = block(mine_dp, depth)
    my_quarter = block(me, quarter)
    done = []

    def begin(copy):
        copy.start()
        done.append(copy)

    token_copies = to_heads(n, ((q, qh), (k, kh), (v, vh)), send_sem, recv_sem, own_sem)
    from_z, halves = [], []
    for o in range(1, nz):
        peer = 2 * lax.rem(z + o, nz) + core
        copy = send_to(
            w.at[:, my_quarter], wf.at[shard, my_quarter], zq_send.at[o], zq_recv.at[o], peer, me
        )
        copy.start()
        from_z.append(copy)
    for o in range(1, nz):
        peer = 2 * lax.rem(z + o, nz) + core
        copy = send_to(w.at[:, upper], wf.at[shard, upper], zh_send.at[o], zh_recv.at[o], peer, me)
        copy.start()
        halves.append(copy)
    begin(pltpu.make_async_copy(w, wf.at[shard], own_sem.at[3]))
    begin(send_to(w, wf.at[shard], core_send.at[0], core_recv.at[0], twin, me))
    begin(
        send_to(
            g.at[:, block(1 - core, half)], g_other, core_send.at[1], core_recv.at[1], twin, me
        )
    )
    for copy in token_copies:
        copy.wait()
    quarters = []
    for o in range(1, nz):
        from_z[o - 1].wait()
        theirs = block(2 * lax.rem(z + nz - o, nz) + core, depth)
        part = wf.at[theirs, my_quarter]
        for p in range(1, n):
            copy = send(part, part, sq_send.at[o, p], sq_recv.at[o, p], lax.rem(me + p, n))
            copy.start()
            quarters.append((o, p, copy))
        begin(send_to(part, part, cq_send.at[o, 0], cq_recv.at[o, 0], twin, me))

    def pass_halves():
        for o in range(1, nz):
            halves[o - 1].wait()
            part = wf.at[block(2 * lax.rem(z + nz - o, nz) + core, depth), upper]
            begin(send_to(part, part, ch_send.at[o], ch_recv.at[o], twin, me))

    def pass_quarters():
        for o, p, copy in quarters:
            copy.wait()
            theirs = block(2 * lax.rem(z + nz - o, nz) + core, depth)
            part = wf.at[theirs, block(lax.rem(me + n - p, n), quarter)]
            begin(send_to(part, part, cq_send.at[o, p], cq_recv.at[o, p], twin, me))

    my_cols = pl.ds(pl.multiple_of(me * width, width), width)
    for t in range(n):
        here = pl.ds(t * rows, rows)
        biases = [tile_bias(near, t, u) for u in window(t, n)]

        def one_head(h, carry):
            cols = pl.ds(pl.multiple_of(h * HEAD, HEAD), HEAD)
            query = qh[here, cols]
            scores = [
                dot_nt(query, kh[pl.ds(u * rows, rows), cols]) * SCALE + bias
                for u, bias in zip(window(t, n), biases)
            ]
            top = functools.reduce(
                jnp.maximum, [jnp.max(s, axis=1, keepdims=True) for s in scores]
            )
            parts = [jnp.exp(s - top) for s in scores]
            total = sum(jnp.sum(p, axis=1, keepdims=True) for p in parts)
            mixed = sum(
                jnp.dot(
                    p.astype(jnp.bfloat16),
                    vh[pl.ds(u * rows, rows), cols],
                    preferred_element_type=jnp.float32,
                )
                for u, p in zip(window(t, n), parts)
            )
            ah[here, cols] = (mixed / total).astype(jnp.bfloat16)
            log_total[h, here, :] = top + jnp.log(total)
            return carry

        lax.fori_loop(0, width // HEAD, one_head, 0)

        @pl.when(me != t)
        def _():
            send(ah.at[here], attn.at[:, my_cols], back_send.at[t], back_recv.at[me], t).start()

        @pl.when(me == t)
        def _():
            pltpu.make_async_copy(ah.at[here], attn.at[:, my_cols], back_own).start()

    for off in range(1, n):
        peer = lax.rem(me + off, n)
        their = pl.ds(pl.multiple_of(peer * rows, rows), rows)
        their_cols = pl.ds(pl.multiple_of(peer * width, width), width)
        send(ah.at[their], attn.at[:, my_cols], back_send.at[peer], back_recv.at[me], peer).wait_send()
        send(
            ah.at[their], attn.at[:, their_cols], back_send.at[peer], back_recv.at[peer], peer
        ).wait_recv()
    mine = pl.ds(pl.multiple_of(me * rows, rows), rows)
    pltpu.make_async_copy(ah.at[mine], attn.at[:, my_cols], back_own).wait()
    begin(send_to(attn, attn_other, core_send.at[2], core_recv.at[2], twin, me))
    pass_quarters()
    pass_halves()
    for copy in done:
        copy.wait()


def backward_kernel(
    n, nz, near, ga, qh, kh, vh, ah, log_total, attn, attn_other, g, g_other, wf,
    dq, dk, dv, gw, mixed, gh, dqh, dkh, dvh, dk_sum, dv_sum,
    wv, gv, px, pz, xin, x_sum, xzin, zin, z_sum, zxin, total,
    send_sem, recv_sem, own_sem, back_send, back_recv, back_own,
    w_sem, xs, xr, xzs, xzr, zs, zr, zxs, zxr, fs, fr, f_own,
):
    z, core, me = place(nz)
    mine_dp = 2 * z + core
    rows = ga.shape[0]
    width = qh.shape[1]
    half = gv.shape[1]
    split = px.shape[3]
    piece = px.shape[2]
    per = n // 2
    heir = 2 * z + me // per
    greet(
        [(mine_dp, lax.rem(me + o, n)) for o in range(1, n)]
        + [(2 * lax.rem(z + o, nz) + core, me) for o in range(1, nz)]
        + [(2 * z + 1 - core, lax.rem(me + o, n)) for o in range(n)]
    )
    copies = to_heads(n, ((ga, gh),), send_sem, recv_sem, own_sem)
    load_g = pltpu.make_async_copy(g.at[:, block(core, half)], gv, w_sem.at[1])
    load_g.start()
    load_w = pltpu.make_async_copy(wf, wv, w_sem.at[0])
    load_w.start()
    dk_sum[...] = jnp.zeros_like(dk_sum)
    dv_sum[...] = jnp.zeros_like(dv_sum)
    load_g.wait()
    z_copies = [
        send_to(
            pz.at[lax.rem(z + o, nz)], zin.at[o], zs.at[o], zr.at[o],
            2 * lax.rem(z + o, nz) + core, me,
        )
        for o in range(1, nz)
    ]
    x_copies = [
        send(px.at[:, lax.rem(me + o, n)], xin.at[o], xs.at[o], xr.at[o], lax.rem(me + o, n))
        for o in range(1, n)
    ]

    def product(i, start):
        cols = block(i, n * piece)
        part = pl.ds(start, split)
        return dot_tn(attn[:, cols], gv[:, part]) + dot_tn(attn_other[:, cols], g_other[:, part])

    def z_part(i, carry):
        pz[i] = product(i, split).astype(jnp.bfloat16).reshape(pz.shape[1:])
        return carry

    def x_part(i, carry):
        px[i] = product(i, 0).astype(jnp.bfloat16).reshape(px.shape[1:])
        return carry

    lax.fori_loop(0, nz, z_part, 0)
    for copy in z_copies:
        copy.start()
    lax.fori_loop(0, nz, x_part, 0)
    for copy in x_copies:
        copy.start()

    def wide(ref):
        return ref.astype(jnp.float32)

    xz_copies = [
        send_to(
            x_sum.at[lax.rem(z + o, nz)], xzin.at[o], xzs.at[o], xzr.at[o],
            2 * lax.rem(z + o, nz) + core, me,
        )
        for o in range(1, nz)
    ]
    zx_copies = [
        send(z_sum.at[lax.rem(me + o, n)], zxin.at[o], zxs.at[o], zxr.at[o], lax.rem(me + o, n))
        for o in range(1, n)
    ]

    def add_x():
        for copy in x_copies:
            copy.wait()
        for i in range(nz):
            x_sum[i] = (
                wide(px[i, me]) + sum(wide(xin[o, i]) for o in range(1, n))
            ).astype(jnp.bfloat16)
        for copy in xz_copies:
            copy.start()

    def add_z():
        for copy in z_copies:
            copy.wait()
        for i in range(n):
            z_sum[i] = (
                wide(pz[z, i]) + sum(wide(zin[o, i]) for o in range(1, nz))
            ).astype(jnp.bfloat16)
        for copy in zx_copies:
            copy.start()

    my_part = gw.at[block(lax.rem(me, per), piece), block(core, half)]

    def shares(start):
        for o in range(n):
            column = lax.rem(me + o, n)
            slot = core * n + me

            def remote():
                copy = send_to(total, my_part, fs.at[o], fr.at[slot], heir, column)
                copy.start() if start else copy.wait_send()

            def local():
                copy = pltpu.make_async_copy(total, my_part, f_own)
                copy.start() if start else copy.wait()

            if o > 0:
                remote()
            else:
                pl.when(heir != mine_dp)(remote)
                pl.when(heir == mine_dp)(local)

    def add_last():
        for copy in xz_copies:
            copy.wait()
        for copy in zx_copies:
            copy.wait()
        total[:, pl.ds(0, split)] = (
            wide(x_sum[z]) + sum(wide(xzin[o]) for o in range(1, nz))
        ).astype(jnp.bfloat16)
        total[:, pl.ds(split, split)] = (
            wide(z_sum[me]) + sum(wide(zxin[o]) for o in range(1, n))
        ).astype(jnp.bfloat16)
        shares(True)

    def take_shares():
        shares(False)
        for c in range(2):
            for j in range(per):
                source = core * per + j
                part = gw.at[pl.ds(j * piece, piece), pl.ds(c * half, half)]

                @pl.when(jnp.logical_or(source != me, core != c))
                def _():
                    send_to(
                        total, part, fs.at[0], fr.at[c * n + source], 2 * z + 1 - core, me
                    ).wait_recv()

    for copy in copies:
        copy.wait()
    my_cols = pl.ds(pl.multiple_of(me * width, width), width)

    def give(a, src, dst, t):
        here = pl.ds(t * rows, rows)

        @pl.when(me != t)
        def _():
            send(
                src.at[here], dst.at[:, my_cols], back_send.at[a, t], back_recv.at[a, me], t
            ).start()

        @pl.when(me == t)
        def _():
            pltpu.make_async_copy(src.at[here], dst.at[:, my_cols], back_own.at[a]).start()

    def give_key(t):
        here = pl.ds(t * rows, rows)
        dkh[here, :] = dk_sum[here, :].astype(jnp.bfloat16)
        dvh[here, :] = dv_sum[here, :].astype(jnp.bfloat16)
        give(1, dkh, dk, t)
        give(2, dvh, dv, t)

    for t in range(n):
        here = pl.ds(t * rows, rows)
        biases = [tile_bias(near, t, u) for u in window(t, n)]

        def one_head(h, carry):
            cols = pl.ds(pl.multiple_of(h * HEAD, HEAD), HEAD)
            query, grad = qh[here, cols], gh[here, cols]
            level = log_total[h, here, :]
            delta = jnp.sum(
                grad.astype(jnp.float32) * ah[here, cols].astype(jnp.float32),
                axis=1,
                keepdims=True,
            )
            out = jnp.zeros((rows, HEAD), jnp.float32)
            for u, bias in zip(window(t, n), biases):
                there = pl.ds(u * rows, rows)
                key, value = kh[there, cols], vh[there, cols]
                weight = jnp.exp(dot_nt(query, key) * SCALE + bias - level)
                dscore = (weight * (dot_nt(grad, value) - delta) * SCALE).astype(jnp.bfloat16)
                out += jnp.dot(dscore, key, preferred_element_type=jnp.float32)
                dk_sum[there, cols] += dot_tn(dscore, query)
                dv_sum[there, cols] += dot_tn(weight.astype(jnp.bfloat16), grad)
            dqh[here, cols] = out.astype(jnp.bfloat16)
            return carry

        lax.fori_loop(0, width // HEAD, one_head, 0)
        give(0, dqh, dq, t)
        if t >= 1:
            give_key(t - 1)
        if t == 1:
            add_x()
        if t == n - 2:
            add_z()
    give_key(n - 1)
    load_w.wait()

    def mix(i, carry):
        cols = block(i, 2 * HEAD)
        mixed[:, cols] = jnp.dot(
            attn[...], wv[:, cols], preferred_element_type=jnp.float32
        ).astype(jnp.bfloat16)
        return carry

    steps = mixed.shape[1] // (2 * HEAD)
    lax.fori_loop(0, steps // 2, mix, 0)
    add_last()
    lax.fori_loop(steps // 2, steps, mix, 0)
    take_shares()
    mine = pl.ds(pl.multiple_of(me * rows, rows), rows)
    for a, (src, dst) in enumerate(((dqh, dq), (dkh, dk), (dvh, dv))):
        for off in range(1, n):
            peer = lax.rem(me + off, n)
            their = pl.ds(pl.multiple_of(peer * rows, rows), rows)
            their_cols = pl.ds(pl.multiple_of(peer * width, width), width)
            send(
                src.at[their], dst.at[:, my_cols], back_send.at[a, peer], back_recv.at[a, me], peer
            ).wait_send()
            send(
                src.at[their],
                dst.at[:, their_cols],
                back_send.at[a, peer],
                back_recv.at[a, peer],
                peer,
            ).wait_recv()
        pltpu.make_async_copy(src.at[mine], dst.at[:, my_cols], back_own.at[a]).wait()


def sems(*shape):
    return pltpu.SemaphoreType.DMA(shape)


def heads_on_device(n, query, key_in, value_in, out_weight, grad_out, neighbours):
    upstream = grad_out[0]
    rows, model_cols = query.shape[1:]
    width = model_cols // n
    heads = width // HEAD
    bf16, f32 = jnp.bfloat16, jnp.float32
    nz = lax.axis_size("dp") // 2
    depth, out_cols = out_weight.shape
    half = out_cols // 2
    split = half // 2
    piece = model_cols // (nz * n)
    hbm = pl.BlockSpec(memory_space=pl.ANY)
    vmem = pl.BlockSpec(memory_space=pltpu.VMEM)
    smem = pl.BlockSpec(memory_space=pltpu.SMEM)
    wide = jax.ShapeDtypeStruct((rows, model_cols), bf16)
    tall = jax.ShapeDtypeStruct((n * rows, width), bf16)
    level = jax.ShapeDtypeStruct((heads, n * rows, 1), f32)
    half_grad = jax.ShapeDtypeStruct((rows, half), bf16)
    full = jax.ShapeDtypeStruct((model_cols, out_cols), bf16)
    attn, attn_other, g_other, weight, qh, kh, vh, ah, log_total = pl.pallas_call(
        functools.partial(forward_kernel, n, nz),
        out_shape=(wide, wide, half_grad, full, tall, tall, tall, tall, level),
        in_specs=[smem] + [hbm] * 5,
        out_specs=(hbm, hbm, hbm, hbm, vmem, vmem, vmem, vmem, vmem),
        scratch_shapes=[
            sems(3, n), sems(3, n), sems(4), sems(n), sems(n), pltpu.SemaphoreType.DMA,
            sems(3), sems(3), sems(nz), sems(nz), sems(nz), sems(nz), sems(nz, n), sems(nz, n),
            sems(nz, n), sems(nz, n), sems(nz), sems(nz),
        ],
        compiler_params=pltpu.CompilerParams(
            collective_id=0, has_side_effects=True, vmem_limit_bytes=50 * 2**20
        ),
        name="attend",
    )(neighbours, query[0], key_in[0], value_in[0], upstream, out_weight)
    grad_attn = dot_nt(upstream, weight).astype(bf16)
    dq, dk, dv, grad_weight, mixed = pl.pallas_call(
        functools.partial(backward_kernel, n, nz),
        out_shape=(
            wide, wide, wide,
            jax.ShapeDtypeStruct((depth, out_cols), bf16),
            jax.ShapeDtypeStruct((rows, out_cols), bf16),
        ),
        in_specs=[smem, hbm] + [vmem] * 7 + [hbm, vmem, hbm],
        out_specs=(hbm, hbm, hbm, hbm, vmem),
        scratch_shapes=[
            pltpu.VMEM(tall.shape, bf16),
            pltpu.VMEM(tall.shape, bf16),
            pltpu.VMEM(tall.shape, bf16),
            pltpu.VMEM(tall.shape, bf16),
            pltpu.VMEM(tall.shape, f32),
            pltpu.VMEM(tall.shape, f32),
            pltpu.VMEM(full.shape, bf16),
            pltpu.VMEM((rows, half), bf16),
            pltpu.VMEM((nz, n, piece, split), bf16),
            pltpu.VMEM((nz, n, piece, split), bf16),
            pltpu.VMEM((n, nz, piece, split), bf16),
            pltpu.VMEM((nz, piece, split), bf16),
            pltpu.VMEM((nz, piece, split), bf16),
            pltpu.VMEM((nz, n, piece, split), bf16),
            pltpu.VMEM((n, piece, split), bf16),
            pltpu.VMEM((n, piece, split), bf16),
            pltpu.VMEM((piece, half), bf16),
            sems(1, n), sems(1, n), sems(1), sems(3, n), sems(3, n), sems(3),
            sems(2), sems(n), sems(n), sems(nz), sems(nz), sems(nz), sems(nz), sems(n), sems(n),
            sems(n), sems(2 * n), pltpu.SemaphoreType.DMA,
        ],
        compiler_params=pltpu.CompilerParams(
            collective_id=1, has_side_effects=True, vmem_limit_bytes=58 * 2**20
        ),
        name="attend_back",
    )(
        neighbours, grad_attn, qh, kh, vh, ah, log_total, attn, attn_other, upstream, g_other,
        weight,
    )
    grad_weight = grad_weight.astype(f32)
    return (mixed[None], dq[None], dk[None], dv[None], grad_weight)


def solution(mesh):
    n = mesh.shape["space"]

    def on_device(query, *rest):
        if query.shape[2] % (n * HEAD) == 0 and n % 2 == 0 and mesh.shape["dp"] % 2 == 0:
            return heads_on_device(n, query, *rest)
        return halo_on_device(query, *rest)

    return jax.shard_map(
        on_device,
        mesh=mesh,
        in_specs=(
            P("dp", "space", None),
            P("dp", "space", None),
            P("dp", "space", None),
            P("dp", None),
            P("dp", "space", None),
            P(),
        ),
        out_specs=(
            P("dp", "space", None),
            P("dp", "space", None),
            P("dp", "space", None),
            P("dp", "space", None),
            P("dp", None),
        ),
        check_vma=False,
    )
```

```python
import functools
import math

import jax
import jax.numpy as jnp
from jax import lax
from jax.experimental import pallas as pl
from jax.experimental.pallas import tpu as pltpu
from jax.sharding import PartitionSpec as P

HEAD = 128


masked_score = -1e30


def padded(x, sides, width):
    for axis, dim in sides:
        size, length = (lax.axis_size(axis), x.shape[dim])
        up = [(i, (i + 1) % size) for i in range(size - 1)]
        down = [(j, i) for i, j in up]
        last = lax.slice_in_dim(x, length - width, length, axis=dim)
        initial = lax.slice_in_dim(x, 0, width, axis=dim)
        before = lax.ppermute(last, axis, up)
        after = lax.ppermute(initial, axis, down)
        x = jnp.concatenate([before, x, after], axis=dim)
    return x


def halo_on_device(query, key_in, value_in, out_weight, grad_out, neighbours):
    query_rows = query[0]
    key_rows = key_in[0]
    value_rows = value_in[0]
    upstream = grad_out[0]
    tile_rows, model_cols = query_rows.shape
    head_count = model_cols // HEAD
    score_scale = 1.0 / math.sqrt(HEAD)
    tile_total = neighbours.shape[0]
    device_tile = lax.axis_index("space")
    window_tiles = device_tile - 1 + jnp.arange(3, dtype=jnp.int32)
    own_list = neighbours[device_tile]
    key_live = jnp.any(
        (own_list[None, :] == window_tiles[:, None]) & (own_list[None, :] >= 0), axis=1
    )
    inside = (window_tiles >= 0) & (window_tiles < tile_total)
    their_lists = neighbours[jnp.clip(window_tiles, 0, tile_total - 1)]
    query_live = inside & jnp.any(their_lists == device_tile, axis=1)
    key_mask = jnp.repeat(key_live, tile_rows)
    query_mask = jnp.repeat(query_live, tile_rows)
    key_value = jnp.stack([key_rows, value_rows])
    kv_near = padded(key_value, (("space", 1),), tile_rows)
    key_heads = kv_near[0].reshape(3 * tile_rows, head_count, HEAD)
    value_heads = kv_near[1].reshape(3 * tile_rows, head_count, HEAD)
    query_heads = query_rows.reshape(tile_rows, head_count, HEAD)
    scores = (
        jnp.einsum("ihd,jhd->hij", query_heads, key_heads, preferred_element_type=jnp.float32)
        * score_scale
    )
    scores = jnp.where(key_mask[None, None, :], scores, masked_score)
    row_max = jnp.max(scores, axis=2, keepdims=True)
    log_total = (row_max + jnp.log(jnp.sum(jnp.exp(scores - row_max), axis=2, keepdims=True)))[
        ..., 0
    ]
    weights = jnp.exp(scores - log_total[..., None])
    weights_bf = weights.astype(jnp.bfloat16)
    attn = (
        jnp.einsum("hij,jhd->ihd", weights_bf, value_heads, preferred_element_type=jnp.float32)
        .reshape(tile_rows, model_cols)
        .astype(jnp.bfloat16)
    )
    shard_piece = lax.all_gather(out_weight, "dp", axis=0, tiled=True)
    attn_cols = attn
    mixed_sum = jnp.dot(attn_cols, shard_piece, preferred_element_type=jnp.float32)
    new_cols = lax.dot_general(
        upstream, shard_piece, (((1,), (1,)), ((), ())), preferred_element_type=jnp.float32
    )
    back_cols = new_cols
    mixed_sum, back_cols = (mixed_sum, back_cols)
    mixed = mixed_sum.astype(jnp.bfloat16)
    grad_attn = back_cols.astype(jnp.bfloat16)
    grad_heads = grad_attn.reshape(tile_rows, head_count, HEAD)
    deltas = jnp.sum(
        grad_heads.astype(jnp.float32)
        * attn.reshape(tile_rows, head_count, HEAD).astype(jnp.float32),
        axis=2,
    ).T
    dprob = jnp.einsum("ihd,jhd->hij", grad_heads, value_heads, preferred_element_type=jnp.float32)
    dscore = (weights * (dprob - deltas[:, :, None]) * score_scale).astype(jnp.bfloat16)
    grad_query = (
        jnp.einsum("hij,jhd->ihd", dscore, key_heads, preferred_element_type=jnp.float32)
        .reshape(tile_rows, model_cols)
        .astype(jnp.bfloat16)
    )
    stat_pair = jnp.stack([log_total, deltas])
    stat_near = padded(stat_pair, (("space", 2),), tile_rows)
    query_grad = jnp.stack([query_rows, grad_attn])
    query_near = padded(query_grad, (("space", 1),), tile_rows)
    far_queries = query_near[0].reshape(3 * tile_rows, head_count, HEAD)
    far_grads = query_near[1].reshape(3 * tile_rows, head_count, HEAD)
    own_keys = key_rows.reshape(tile_rows, head_count, HEAD)
    own_values = value_rows.reshape(tile_rows, head_count, HEAD)
    back_scores = (
        jnp.einsum("jhd,ihd->hji", far_queries, own_keys, preferred_element_type=jnp.float32)
        * score_scale
    )
    back_weights = jnp.where(
        query_mask[None, :, None], jnp.exp(back_scores - stat_near[0][:, :, None]), 0.0
    )
    back_bf = back_weights.astype(jnp.bfloat16)
    grad_value = (
        jnp.einsum("hji,jhd->ihd", back_bf, far_grads, preferred_element_type=jnp.float32)
        .reshape(tile_rows, model_cols)
        .astype(jnp.bfloat16)
    )
    back_dprob = jnp.einsum(
        "jhd,ihd->hji", far_grads, own_values, preferred_element_type=jnp.float32
    )
    back_dscore = (back_weights * (back_dprob - stat_near[1][:, :, None]) * score_scale).astype(
        jnp.bfloat16
    )
    grad_key = (
        jnp.einsum("hji,jhd->ihd", back_dscore, far_queries, preferred_element_type=jnp.float32)
        .reshape(tile_rows, model_cols)
        .astype(jnp.bfloat16)
    )
    attn_cols = attn
    partial_rows = lax.psum_scatter(
        lax.dot_general(
            attn_cols, upstream, (((0,), (0,)), ((), ())), preferred_element_type=jnp.float32
        ),
        ("dp", "space"),
        scatter_dimension=0,
        tiled=True,
    )
    grad_weight = lax.all_gather(partial_rows, "space", axis=0, tiled=True)
    return (mixed[None], grad_query[None], grad_key[None], grad_value[None], grad_weight)


MESH = pl.DeviceIdType.MESH
SCALE = 1.0 / math.sqrt(HEAD)


def window(tile, tiles):
    return range(max(0, tile - 1), min(tiles, tile + 2))


def tile_bias(near, tile, other):
    live = near[tile, 0] == other
    for slot in range(1, near.shape[1]):
        live = jnp.logical_or(live, near[tile, slot] == other)
    return jnp.where(live, 0.0, masked_score).astype(jnp.float32)


def dot_nt(a, b):
    return lax.dot_general(a, b, (((1,), (1,)), ((), ())), preferred_element_type=jnp.float32)


def dot_tn(a, b):
    return lax.dot_general(a, b, (((0,), (0,)), ((), ())), preferred_element_type=jnp.float32)


def place(nz):
    row = lax.axis_index("dp")
    return row // 2, row % 2, lax.axis_index("space")


def greet(peers):
    barrier = pltpu.get_barrier_semaphore()
    for row, column in peers:
        pl.semaphore_signal(
            barrier, inc=1, device_id={"dp": row, "space": column}, device_id_type=MESH
        )
    pl.semaphore_wait(barrier, len(peers))


def send_to(src, dst, send_sem, recv_sem, row, column):
    return pltpu.make_async_remote_copy(
        src_ref=src,
        dst_ref=dst,
        send_sem=send_sem,
        recv_sem=recv_sem,
        device_id={"dp": row, "space": column},
        device_id_type=MESH,
    )


def send(src, dst, send_sem, recv_sem, peer):
    return send_to(src, dst, send_sem, recv_sem, lax.axis_index("dp"), peer)


def block(index, size):
    return pl.ds(pl.multiple_of(index * size, size), size)


def layer_kernel(
    n, nz, near, q, k, v, g, w, dq, dk, dv, gw, mixed,
    attn, attn_other, gv, g_other, wf, ga, qh, kh, vh, ah, gh, dqh, dkh, dvh,
    log_total, dk_sum, dv_sum, px, pz, xin, x_sum, xzin, zin, z_sum, zxin, total,
    send_sem, recv_sem, own_sem, back_send, back_recv, back_own, load_sem,
    core_send, core_recv, zq_send, zq_recv, zh_send, zh_recv, sq_send, sq_recv,
    cq_send, cq_recv, ch_send, ch_recv,
    xs, xr, xzs, xzr, zs, zr, zxs, zxr, fs, fr, f_own,
):
    z, core, me = place(nz)
    mine_dp = 2 * z + core
    twin = 2 * z + 1 - core
    rows = q.shape[0]
    width = qh.shape[1]
    heads = width // HEAD
    depth, model = w.shape
    half = model // 2
    quarter = half // n
    split = px.shape[3]
    rest = pz.shape[3]
    piece = px.shape[2]
    per = n // 2
    heir = 2 * z + me // per
    upper = pl.ds(half, half)
    shard = block(mine_dp, depth)
    my_quarter = block(me, quarter)
    mine = block(me, rows)
    bf16 = jnp.bfloat16

    def column(o):
        return lax.rem(me + o, n)

    def line(o):
        return 2 * lax.rem(z + o, nz) + core

    def wide(ref):
        return ref.astype(jnp.float32)

    greet(
        [(mine_dp, column(o)) for o in range(1, n)]
        + [(line(o), me) for o in range(1, nz)]
        + [(twin, column(o)) for o in range(n)]
    )
    done = []

    def begin(copy):
        copy.start()
        done.append(copy)

    def out_copy(a, src, dst, o, h):
        peer = column(o)
        return send(
            src.at[:, block(peer * heads + h, HEAD)], dst.at[mine, block(h, HEAD)],
            send_sem.at[a, o, h], recv_sem.at[a, o, h], peer,
        )

    def out_own(a, src, dst, h):
        return pltpu.make_async_copy(
            src.at[:, block(me * heads + h, HEAD)], dst.at[mine, block(h, HEAD)], own_sem.at[a, h]
        )

    def back_copy(a, src, dst, o, h):
        peer = column(o)
        return send(
            src.at[block(peer, rows), block(h, HEAD)], dst.at[:, block(me * heads + h, HEAD)],
            back_send.at[a, o, h], back_recv.at[a, o, h], peer,
        )

    def back_local(a, src, dst, h):
        return pltpu.make_async_copy(
            src.at[mine, block(h, HEAD)], dst.at[:, block(me * heads + h, HEAD)], back_own.at[a, h]
        )

    def give(a, src, dst, h):
        for o in range(1, n):
            back_copy(a, src, dst, o, h).start()
        back_local(a, src, dst, h).start()

    def take(a, src, dst, h):
        for o in range(1, n):
            back_copy(a, src, dst, o, h).wait()
        back_local(a, src, dst, h).wait()

    inputs = ((q, qh), (k, kh), (v, vh))

    def start_head(h, carry):
        for a, (src, dst) in enumerate(inputs):
            for o in range(1, n):
                out_copy(a, src, dst, o, h).start()
            out_own(a, src, dst, h).start()
        return carry

    lax.fori_loop(0, 1, start_head, 0)
    from_z, halves, quarters = [], [], []
    for o in range(1, nz):
        copy = send_to(
            w.at[:, my_quarter], wf.at[shard, my_quarter], zq_send.at[o], zq_recv.at[o],
            line(o), me,
        )
        copy.start()
        from_z.append(copy)
    lax.fori_loop(1, heads, start_head, 0)
    for o in range(1, nz):
        copy = send_to(
            w.at[:, upper], wf.at[shard, upper], zh_send.at[o], zh_recv.at[o], line(o), me
        )
        copy.start()
        halves.append(copy)
    load_g = pltpu.make_async_copy(g, gv, load_sem.at[0])
    load_g.start()
    begin(pltpu.make_async_copy(w, wf.at[shard], load_sem.at[1]))
    begin(send_to(w, wf.at[shard], core_send.at[0], core_recv.at[0], twin, me))
    other_g = send_to(
        g.at[:, block(1 - core, half)], g_other, core_send.at[1], core_recv.at[1], twin, me
    )
    other_g.start()

    def theirs(o):
        return block(line(nz - o), depth)

    def pass_from_z():
        for o in range(1, nz):
            from_z[o - 1].wait()
            part = wf.at[theirs(o), my_quarter]
            for p in range(1, n):
                send(part, part, sq_send.at[o, p], sq_recv.at[o, p], column(p)).start()
            send_to(part, part, cq_send.at[o, 0], cq_recv.at[o, 0], twin, me).start()

    def pass_quarters():
        for o in range(1, nz):
            part = wf.at[theirs(o), my_quarter]
            for p in range(1, n):
                send(part, part, sq_send.at[o, p], sq_recv.at[o, p], column(p)).wait()
                came = wf.at[theirs(o), block(column(n - p), quarter)]
                begin(send_to(came, came, cq_send.at[o, p], cq_recv.at[o, p], twin, me))
            done.append(send_to(part, part, cq_send.at[o, 0], cq_recv.at[o, 0], twin, me))

    def pass_halves():
        for o in range(1, nz):
            halves[o - 1].wait()
            part = wf.at[theirs(o), upper]
            begin(send_to(part, part, ch_send.at[o], ch_recv.at[o], twin, me))

    def forward_head(h, carry):
        for a, (src, dst) in enumerate(inputs):
            for o in range(1, n):
                out_copy(a, src, dst, o, h).wait()
            out_own(a, src, dst, h).wait()
        cols = block(h, HEAD)
        for t in range(n):
            here = pl.ds(t * rows, rows)
            query = qh[here, cols]
            scores = [
                dot_nt(query, kh[pl.ds(u * rows, rows), cols]) * SCALE + tile_bias(near, t, u)
                for u in window(t, n)
            ]
            top = functools.reduce(
                jnp.maximum, [jnp.max(s, axis=1, keepdims=True) for s in scores]
            )
            parts = [jnp.exp(s - top) for s in scores]
            summed = sum(jnp.sum(p, axis=1, keepdims=True) for p in parts)
            out = sum(
                jnp.dot(
                    p.astype(bf16),
                    vh[pl.ds(u * rows, rows), cols],
                    preferred_element_type=jnp.float32,
                )
                for u, p in zip(window(t, n), parts)
            )
            ah[here, cols] = (out / summed).astype(bf16)
            log_total[h, here, :] = top + jnp.log(summed)
        give(0, ah, attn, h)
        pl.when(h == 0)(pass_from_z)
        return carry

    lax.fori_loop(0, heads, forward_head, 0)
    for h in range(heads):
        take(0, ah, attn, h)
    other_attn = send_to(attn, attn_other, core_send.at[2], core_recv.at[2], twin, me)
    other_attn.start()
    load_g.wait()
    other_g.wait()
    other_attn.wait()

    def z_copy(o):
        return send_to(
            pz.at[lax.rem(z + o, nz)], zin.at[o], zs.at[o], zr.at[o], line(o), me
        )

    x_copies = [
        send(px.at[:, column(o)], xin.at[o], xs.at[o], xr.at[o], column(o)) for o in range(1, n)
    ]

    def product(i, start, size):
        cols = block(i, n * piece)
        ours = gv[:, pl.ds(pl.multiple_of(core * half + start, HEAD), size)]
        return dot_tn(attn[:, cols], ours) + dot_tn(
            attn_other[:, cols], g_other[:, pl.ds(start, size)]
        )

    def z_part(i, carry):
        o = i + 1
        to = lax.rem(z + o, nz)
        pz[to] = product(to, split, rest).astype(bf16).reshape(pz.shape[1:])

        @pl.when(o < nz)
        def _():
            z_copy(o).start()

        return carry

    def x_part(i, carry):
        px[i] = product(i, 0, split).astype(bf16).reshape(px.shape[1:])
        return carry

    lax.fori_loop(0, nz, z_part, 0)
    pass_quarters()
    lax.fori_loop(0, nz, x_part, 0)
    for copy in x_copies:
        copy.start()
    pass_halves()
    for copy in done:
        copy.wait()

    def project_back(i, carry):
        o = i + 1
        to = lax.rem(me + o, n)
        cols = block(to, width)
        ga[:, cols] = dot_nt(gv[...], wf[cols, :]).astype(bf16)

        @pl.when(o < n)
        def _():
            for h in range(heads):
                out_copy(3, ga, gh, o, h).start()

        @pl.when(o == n)
        def _():
            for h in range(heads):
                out_own(3, ga, gh, h).start()

        return carry

    lax.fori_loop(0, n, project_back, 0)

    def mix(i, carry):
        cols = block(i, 2 * HEAD)
        mixed[:, cols] = jnp.dot(
            attn[...], wf[:, cols], preferred_element_type=jnp.float32
        ).astype(bf16)
        return carry

    steps = model // (2 * HEAD)
    lax.fori_loop(0, steps // 2, mix, 0)

    def xz_copy(o):
        return send_to(
            x_sum.at[lax.rem(z + o, nz)], xzin.at[o], xzs.at[o], xzr.at[o], line(o), me
        )

    def add_x():
        for copy in x_copies:
            copy.wait()
        for i in range(nz):
            x_sum[i] = (
                wide(px[i, me]) + sum(wide(xin[o, i]) for o in range(1, n))
            ).astype(bf16)
        for o in range(1, nz):
            xz_copy(o).start()

    def backward_head(h, carry):
        for o in range(1, n):
            out_copy(3, ga, gh, o, h).wait()
        out_own(3, ga, gh, h).wait()
        cols = block(h, HEAD)
        dk_sum[...] = jnp.zeros_like(dk_sum)
        dv_sum[...] = jnp.zeros_like(dv_sum)
        for t in range(n):
            here = pl.ds(t * rows, rows)
            query, grad = qh[here, cols], gh[here, cols]
            level = log_total[h, here, :]
            delta = jnp.sum(wide(grad) * wide(ah[here, cols]), axis=1, keepdims=True)
            out = jnp.zeros((rows, HEAD), jnp.float32)
            for u in window(t, n):
                there = pl.ds(u * rows, rows)
                key, value = kh[there, cols], vh[there, cols]
                weight = jnp.exp(dot_nt(query, key) * SCALE + tile_bias(near, t, u) - level)
                dscore = (weight * (dot_nt(grad, value) - delta) * SCALE).astype(bf16)
                out += jnp.dot(dscore, key, preferred_element_type=jnp.float32)
                dk_sum[there, :] += dot_tn(dscore, query)
                dv_sum[there, :] += dot_tn(weight.astype(bf16), grad)
            dqh[here, cols] = out.astype(bf16)
        give(1, dqh, dq, h)
        dkh[:, cols] = dk_sum[...].astype(bf16)
        give(2, dkh, dk, h)
        dvh[:, cols] = dv_sum[...].astype(bf16)
        give(3, dvh, dv, h)
        pl.when(h == 0)(add_x)
        return carry

    lax.fori_loop(0, heads, backward_head, 0)
    for o in range(1, nz):
        z_copy(o).wait()
    for i in range(n):
        z_sum[i] = (wide(pz[z, i]) + sum(wide(zin[o, i]) for o in range(1, nz))).astype(bf16)
    zx_copies = [
        send(z_sum.at[column(o)], zxin.at[o], zxs.at[o], zxr.at[o], column(o))
        for o in range(1, n)
    ]
    for copy in zx_copies:
        copy.start()
    lax.fori_loop(steps // 2, steps, mix, 0)
    for o in range(1, nz):
        xz_copy(o).wait()
    for copy in zx_copies:
        copy.wait()
    total[:, pl.ds(0, split)] = (
        wide(x_sum[z]) + sum(wide(xzin[o]) for o in range(1, nz))
    ).astype(bf16)
    total[:, pl.ds(split, rest)] = (
        wide(z_sum[me]) + sum(wide(zxin[o]) for o in range(1, n))
    ).astype(bf16)
    my_part = gw.at[block(lax.rem(me, per), piece), block(core, half)]

    def shares(start):
        for o in range(n):

            def remote():
                copy = send_to(total, my_part, fs.at[o], fr.at[core * n + me], heir, column(o))
                copy.start() if start else copy.wait_send()

            def local():
                copy = pltpu.make_async_copy(total, my_part, f_own)
                copy.start() if start else copy.wait()

            if o > 0:
                remote()
            else:
                pl.when(heir != mine_dp)(remote)
                pl.when(heir == mine_dp)(local)

    shares(True)
    for h in range(heads):
        take(1, dqh, dq, h)
        take(2, dkh, dk, h)
        take(3, dvh, dv, h)
    shares(False)
    for c in range(2):
        for j in range(per):
            source = core * per + j
            part = gw.at[pl.ds(j * piece, piece), pl.ds(c * half, half)]

            @pl.when(jnp.logical_or(source != me, core != c))
            def _():
                send_to(total, part, fs.at[0], fr.at[c * n + source], twin, me).wait_recv()


def sems(*shape):
    return pltpu.SemaphoreType.DMA(shape)


def heads_on_device(n, query, key_in, value_in, out_weight, grad_out, neighbours):
    upstream = grad_out[0]
    rows, model_cols = query.shape[1:]
    width = model_cols // n
    heads = width // HEAD
    bf16, f32 = jnp.bfloat16, jnp.float32
    nz = lax.axis_size("dp") // 2
    depth, out_cols = out_weight.shape
    half = out_cols // 2
    split = half // (3 * HEAD) * HEAD
    piece = model_cols // (nz * n)
    hbm = pl.BlockSpec(memory_space=pl.ANY)
    vmem = pl.BlockSpec(memory_space=pltpu.VMEM)
    smem = pl.BlockSpec(memory_space=pltpu.SMEM)
    wide = jax.ShapeDtypeStruct((rows, model_cols), bf16)
    tall = pltpu.VMEM((n * rows, width), bf16)
    sums = pltpu.VMEM((n * rows, HEAD), f32)
    rest = half - split
    dq, dk, dv, grad_weight, mixed = pl.pallas_call(
        functools.partial(layer_kernel, n, nz),
        out_shape=(
            wide, wide, wide,
            jax.ShapeDtypeStruct((depth, out_cols), bf16),
            jax.ShapeDtypeStruct((rows, out_cols), bf16),
        ),
        in_specs=[smem] + [hbm] * 5,
        out_specs=(hbm, hbm, hbm, hbm, vmem),
        scratch_shapes=[
            pltpu.VMEM((rows, model_cols), bf16),
            pltpu.VMEM((rows, model_cols), bf16),
            pltpu.VMEM((rows, out_cols), bf16),
            pltpu.VMEM((rows, half), bf16),
            pltpu.VMEM((model_cols, out_cols), bf16),
            pltpu.VMEM((rows, model_cols), bf16),
            tall, tall, tall, tall, tall, tall, tall, tall,
            pltpu.VMEM((heads, n * rows, 1), f32),
            sums, sums,
            pltpu.VMEM((nz, n, piece, split), bf16),
            pltpu.VMEM((nz, n, piece, rest), bf16),
            pltpu.VMEM((n, nz, piece, split), bf16),
            pltpu.VMEM((nz, piece, split), bf16),
            pltpu.VMEM((nz, piece, split), bf16),
            pltpu.VMEM((nz, n, piece, rest), bf16),
            pltpu.VMEM((n, piece, rest), bf16),
            pltpu.VMEM((n, piece, rest), bf16),
            pltpu.VMEM((piece, half), bf16),
            sems(4, n, heads), sems(4, n, heads), sems(4, heads),
            sems(4, n, heads), sems(4, n, heads), sems(4, heads), sems(2),
            sems(3), sems(3), sems(nz), sems(nz), sems(nz), sems(nz), sems(nz, n), sems(nz, n),
            sems(nz, n), sems(nz, n), sems(nz), sems(nz),
            sems(n), sems(n), sems(nz), sems(nz), sems(nz), sems(nz), sems(n), sems(n),
            sems(n), sems(2 * n), pltpu.SemaphoreType.DMA,
        ],
        compiler_params=pltpu.CompilerParams(
            collective_id=0, has_side_effects=True, vmem_limit_bytes=60 * 2**20
        ),
        name="layer",
    )(neighbours, query[0], key_in[0], value_in[0], upstream, out_weight)
    grad_weight = grad_weight.astype(f32)
    return (mixed[None], dq[None], dk[None], dv[None], grad_weight)


def solution(mesh):
    n = mesh.shape["space"]

    def on_device(query, *rest):
        if query.shape[2] % (n * HEAD) == 0 and n % 2 == 0 and mesh.shape["dp"] % 2 == 0:
            return heads_on_device(n, query, *rest)
        return halo_on_device(query, *rest)

    return jax.shard_map(
        on_device,
        mesh=mesh,
        in_specs=(
            P("dp", "space", None),
            P("dp", "space", None),
            P("dp", "space", None),
            P("dp", None),
            P("dp", "space", None),
            P(),
        ),
        out_specs=(
            P("dp", "space", None),
            P("dp", "space", None),
            P("dp", "space", None),
            P("dp", "space", None),
            P("dp", None),
        ),
        check_vma=False,
    )
```

```python
import functools
import math

import jax
import jax.numpy as jnp
from jax import lax
from jax.experimental import pallas as pl
from jax.experimental.pallas import tpu as pltpu
from jax.sharding import PartitionSpec as P

HEAD = 128


masked_score = -1e30


def padded(x, sides, width):
    for axis, dim in sides:
        size, length = (lax.axis_size(axis), x.shape[dim])
        up = [(i, (i + 1) % size) for i in range(size - 1)]
        down = [(j, i) for i, j in up]
        last = lax.slice_in_dim(x, length - width, length, axis=dim)
        initial = lax.slice_in_dim(x, 0, width, axis=dim)
        before = lax.ppermute(last, axis, up)
        after = lax.ppermute(initial, axis, down)
        x = jnp.concatenate([before, x, after], axis=dim)
    return x


def halo_on_device(query, key_in, value_in, out_weight, grad_out, neighbours):
    query_rows = query[0]
    key_rows = key_in[0]
    value_rows = value_in[0]
    upstream = grad_out[0]
    tile_rows, model_cols = query_rows.shape
    head_count = model_cols // HEAD
    score_scale = 1.0 / math.sqrt(HEAD)
    tile_total = neighbours.shape[0]
    device_tile = lax.axis_index("space")
    window_tiles = device_tile - 1 + jnp.arange(3, dtype=jnp.int32)
    own_list = neighbours[device_tile]
    key_live = jnp.any(
        (own_list[None, :] == window_tiles[:, None]) & (own_list[None, :] >= 0), axis=1
    )
    inside = (window_tiles >= 0) & (window_tiles < tile_total)
    their_lists = neighbours[jnp.clip(window_tiles, 0, tile_total - 1)]
    query_live = inside & jnp.any(their_lists == device_tile, axis=1)
    key_mask = jnp.repeat(key_live, tile_rows)
    query_mask = jnp.repeat(query_live, tile_rows)
    key_value = jnp.stack([key_rows, value_rows])
    kv_near = padded(key_value, (("space", 1),), tile_rows)
    key_heads = kv_near[0].reshape(3 * tile_rows, head_count, HEAD)
    value_heads = kv_near[1].reshape(3 * tile_rows, head_count, HEAD)
    query_heads = query_rows.reshape(tile_rows, head_count, HEAD)
    scores = (
        jnp.einsum("ihd,jhd->hij", query_heads, key_heads, preferred_element_type=jnp.float32)
        * score_scale
    )
    scores = jnp.where(key_mask[None, None, :], scores, masked_score)
    row_max = jnp.max(scores, axis=2, keepdims=True)
    log_total = (row_max + jnp.log(jnp.sum(jnp.exp(scores - row_max), axis=2, keepdims=True)))[
        ..., 0
    ]
    weights = jnp.exp(scores - log_total[..., None])
    weights_bf = weights.astype(jnp.bfloat16)
    attn = (
        jnp.einsum("hij,jhd->ihd", weights_bf, value_heads, preferred_element_type=jnp.float32)
        .reshape(tile_rows, model_cols)
        .astype(jnp.bfloat16)
    )
    shard_piece = lax.all_gather(out_weight, "dp", axis=0, tiled=True)
    attn_cols = attn
    mixed_sum = jnp.dot(attn_cols, shard_piece, preferred_element_type=jnp.float32)
    new_cols = lax.dot_general(
        upstream, shard_piece, (((1,), (1,)), ((), ())), preferred_element_type=jnp.float32
    )
    back_cols = new_cols
    mixed_sum, back_cols = (mixed_sum, back_cols)
    mixed = mixed_sum.astype(jnp.bfloat16)
    grad_attn = back_cols.astype(jnp.bfloat16)
    grad_heads = grad_attn.reshape(tile_rows, head_count, HEAD)
    deltas = jnp.sum(
        grad_heads.astype(jnp.float32)
        * attn.reshape(tile_rows, head_count, HEAD).astype(jnp.float32),
        axis=2,
    ).T
    dprob = jnp.einsum("ihd,jhd->hij", grad_heads, value_heads, preferred_element_type=jnp.float32)
    dscore = (weights * (dprob - deltas[:, :, None]) * score_scale).astype(jnp.bfloat16)
    grad_query = (
        jnp.einsum("hij,jhd->ihd", dscore, key_heads, preferred_element_type=jnp.float32)
        .reshape(tile_rows, model_cols)
        .astype(jnp.bfloat16)
    )
    stat_pair = jnp.stack([log_total, deltas])
    stat_near = padded(stat_pair, (("space", 2),), tile_rows)
    query_grad = jnp.stack([query_rows, grad_attn])
    query_near = padded(query_grad, (("space", 1),), tile_rows)
    far_queries = query_near[0].reshape(3 * tile_rows, head_count, HEAD)
    far_grads = query_near[1].reshape(3 * tile_rows, head_count, HEAD)
    own_keys = key_rows.reshape(tile_rows, head_count, HEAD)
    own_values = value_rows.reshape(tile_rows, head_count, HEAD)
    back_scores = (
        jnp.einsum("jhd,ihd->hji", far_queries, own_keys, preferred_element_type=jnp.float32)
        * score_scale
    )
    back_weights = jnp.where(
        query_mask[None, :, None], jnp.exp(back_scores - stat_near[0][:, :, None]), 0.0
    )
    back_bf = back_weights.astype(jnp.bfloat16)
    grad_value = (
        jnp.einsum("hji,jhd->ihd", back_bf, far_grads, preferred_element_type=jnp.float32)
        .reshape(tile_rows, model_cols)
        .astype(jnp.bfloat16)
    )
    back_dprob = jnp.einsum(
        "jhd,ihd->hji", far_grads, own_values, preferred_element_type=jnp.float32
    )
    back_dscore = (back_weights * (back_dprob - stat_near[1][:, :, None]) * score_scale).astype(
        jnp.bfloat16
    )
    grad_key = (
        jnp.einsum("hji,jhd->ihd", back_dscore, far_queries, preferred_element_type=jnp.float32)
        .reshape(tile_rows, model_cols)
        .astype(jnp.bfloat16)
    )
    attn_cols = attn
    partial_rows = lax.psum_scatter(
        lax.dot_general(
            attn_cols, upstream, (((0,), (0,)), ((), ())), preferred_element_type=jnp.float32
        ),
        ("dp", "space"),
        scatter_dimension=0,
        tiled=True,
    )
    grad_weight = lax.all_gather(partial_rows, "space", axis=0, tiled=True)
    return (mixed[None], grad_query[None], grad_key[None], grad_value[None], grad_weight)


MESH = pl.DeviceIdType.MESH
SCALE = 1.0 / math.sqrt(HEAD)


def window(tile, tiles):
    return range(max(0, tile - 1), min(tiles, tile + 2))


def tile_bias(near, tile, other):
    live = near[tile, 0] == other
    for slot in range(1, near.shape[1]):
        live = jnp.logical_or(live, near[tile, slot] == other)
    return jnp.where(live, 0.0, masked_score).astype(jnp.float32)


def dot_nt(a, b):
    return lax.dot_general(a, b, (((1,), (1,)), ((), ())), preferred_element_type=jnp.float32)


def dot_tn(a, b):
    return lax.dot_general(a, b, (((0,), (0,)), ((), ())), preferred_element_type=jnp.float32)


def place(nz):
    row = lax.axis_index("dp")
    return row // 2, row % 2, lax.axis_index("space")


def greet(peers):
    barrier = pltpu.get_barrier_semaphore()
    for row, column in peers:
        pl.semaphore_signal(
            barrier, inc=1, device_id={"dp": row, "space": column}, device_id_type=MESH
        )
    pl.semaphore_wait(barrier, len(peers))


def send_to(src, dst, send_sem, recv_sem, row, column):
    return pltpu.make_async_remote_copy(
        src_ref=src,
        dst_ref=dst,
        send_sem=send_sem,
        recv_sem=recv_sem,
        device_id={"dp": row, "space": column},
        device_id_type=MESH,
    )


def send(src, dst, send_sem, recv_sem, peer):
    return send_to(src, dst, send_sem, recv_sem, lax.axis_index("dp"), peer)


def block(index, size):
    return pl.ds(pl.multiple_of(index * size, size), size)


def layer_kernel(
    n, nz, near, q, k, v, g, w, dq, dk, dv, gw, mixed,
    attn, attn_other, gv, g_other, wf, ga, qh, kh, vh, ah, gh, dqh, dkh, dvh,
    log_total, dk_sum, dv_sum, px, pz, xin, x_sum, xzin, zin, z_sum, zxin, total,
    send_sem, recv_sem, own_sem, back_send, back_recv, back_own, load_sem,
    core_send, core_recv, zq_send, zq_recv, zh_send, zh_recv, sq_send, sq_recv,
    cq_send, cq_recv, ch_send, ch_recv,
    xs, xr, xzs, xzr, zs, zr, zxs, zxr, fs, fr, f_own,
):
    z, core, me = place(nz)
    mine_dp = 2 * z + core
    twin = 2 * z + 1 - core
    rows = q.shape[0]
    width = qh.shape[1]
    heads = width // HEAD
    depth, model = w.shape
    half = model // 2
    quarter = half // n
    split = px.shape[3]
    rest = pz.shape[3]
    piece = px.shape[2]
    per = n // 2
    heir = 2 * z + me // per
    upper = pl.ds(half, half)
    shard = block(mine_dp, depth)
    my_quarter = block(me, quarter)
    mine = block(me, rows)
    bf16 = jnp.bfloat16

    def column(o):
        return lax.rem(me + o, n)

    def line(o):
        return 2 * lax.rem(z + o, nz) + core

    def wide(ref):
        return ref.astype(jnp.float32)

    greet(
        [(mine_dp, column(o)) for o in range(1, n)]
        + [(line(o), me) for o in range(1, nz)]
        + [(twin, column(o)) for o in range(n)]
    )
    done = []

    def begin(copy):
        copy.start()
        done.append(copy)

    def out_copy(a, src, dst, o, h):
        peer = column(o)
        return send(
            src.at[:, block(peer * heads + h, HEAD)], dst.at[mine, block(h, HEAD)],
            send_sem.at[a, o, h], recv_sem.at[a, o, h], peer,
        )

    def out_own(a, src, dst, h):
        return pltpu.make_async_copy(
            src.at[:, block(me * heads + h, HEAD)], dst.at[mine, block(h, HEAD)], own_sem.at[a, h]
        )

    def back_copy(a, src, dst, o, h):
        peer = column(o)
        return send(
            src.at[block(peer, rows), block(h, HEAD)], dst.at[:, block(me * heads + h, HEAD)],
            back_send.at[a, o, h], back_recv.at[a, o, h], peer,
        )

    def back_local(a, src, dst, h):
        return pltpu.make_async_copy(
            src.at[mine, block(h, HEAD)], dst.at[:, block(me * heads + h, HEAD)], back_own.at[a, h]
        )

    def give(a, src, dst, h):
        for o in range(1, n):
            back_copy(a, src, dst, o, h).start()
        back_local(a, src, dst, h).start()

    def take(a, src, dst, h):
        for o in range(1, n):
            back_copy(a, src, dst, o, h).wait()
        back_local(a, src, dst, h).wait()

    inputs = ((q, qh), (k, kh), (v, vh))

    def start_head(h, carry):
        for a, (src, dst) in enumerate(inputs):
            for o in range(1, n):
                out_copy(a, src, dst, o, h).start()
            out_own(a, src, dst, h).start()
        return carry

    lax.fori_loop(0, 1, start_head, 0)
    from_z, halves, quarters = [], [], []
    for o in range(1, nz):
        copy = send_to(
            w.at[:, my_quarter], wf.at[shard, my_quarter], zq_send.at[o], zq_recv.at[o],
            line(o), me,
        )
        copy.start()
        from_z.append(copy)
    lax.fori_loop(1, heads, start_head, 0)
    for o in range(1, nz):
        copy = send_to(
            w.at[:, upper], wf.at[shard, upper], zh_send.at[o], zh_recv.at[o], line(o), me
        )
        copy.start()
        halves.append(copy)
    load_g = pltpu.make_async_copy(g, gv, load_sem.at[0])
    load_g.start()
    begin(pltpu.make_async_copy(w, wf.at[shard], load_sem.at[1]))
    begin(send_to(w, wf.at[shard], core_send.at[0], core_recv.at[0], twin, me))
    other_g = send_to(
        g.at[:, block(1 - core, half)], g_other, core_send.at[1], core_recv.at[1], twin, me
    )
    other_g.start()

    def theirs(o):
        return block(line(nz - o), depth)

    def pass_from_z():
        for o in range(1, nz):
            from_z[o - 1].wait()
            part = wf.at[theirs(o), my_quarter]
            for p in range(1, n):
                send(part, part, sq_send.at[o, p], sq_recv.at[o, p], column(p)).start()
            send_to(part, part, cq_send.at[o, 0], cq_recv.at[o, 0], twin, me).start()

    def pass_quarters():
        for o in range(1, nz):
            part = wf.at[theirs(o), my_quarter]
            for p in range(1, n):
                send(part, part, sq_send.at[o, p], sq_recv.at[o, p], column(p)).wait()
                came = wf.at[theirs(o), block(column(n - p), quarter)]
                begin(send_to(came, came, cq_send.at[o, p], cq_recv.at[o, p], twin, me))
            done.append(send_to(part, part, cq_send.at[o, 0], cq_recv.at[o, 0], twin, me))

    def pass_halves():
        for o in range(1, nz):
            halves[o - 1].wait()
            part = wf.at[theirs(o), upper]
            begin(send_to(part, part, ch_send.at[o], ch_recv.at[o], twin, me))

    def forward_head(h, carry):
        for a, (src, dst) in enumerate(inputs):
            for o in range(1, n):
                out_copy(a, src, dst, o, h).wait()
            out_own(a, src, dst, h).wait()
        cols = block(h, HEAD)
        for t in range(n):
            here = pl.ds(t * rows, rows)
            query = qh[here, cols]
            scores = [
                dot_nt(kh[pl.ds(u * rows, rows), cols], query) * SCALE + tile_bias(near, t, u)
                for u in window(t, n)
            ]
            top = functools.reduce(
                jnp.maximum, [jnp.max(s, axis=0, keepdims=True) for s in scores]
            )
            parts = [jnp.exp(s - top) for s in scores]
            summed = sum(jnp.sum(p, axis=0, keepdims=True) for p in parts)
            out = sum(
                dot_tn(vh[pl.ds(u * rows, rows), cols], p.astype(bf16))
                for u, p in zip(window(t, n), parts)
            )
            ah[here, cols] = jnp.transpose(out / summed).astype(bf16)
            log_total[h, t] = top + jnp.log(summed)
        give(0, ah, attn, h)
        pl.when(h == heads - 1)(pass_from_z)
        return carry

    lax.fori_loop(0, heads, forward_head, 0)
    for h in range(heads):
        take(0, ah, attn, h)
    other_attn = send_to(attn, attn_other, core_send.at[2], core_recv.at[2], twin, me)
    other_attn.start()
    load_g.wait()
    other_g.wait()
    other_attn.wait()

    def z_copy(o):
        return send_to(
            pz.at[lax.rem(z + o, nz)], zin.at[o], zs.at[o], zr.at[o], line(o), me
        )

    x_copies = [
        send(px.at[:, column(o)], xin.at[o], xs.at[o], xr.at[o], column(o)) for o in range(1, n)
    ]

    def product(i, start, size):
        cols = block(i, n * piece)
        ours = gv[:, pl.ds(pl.multiple_of(core * half + start, HEAD), size)]
        return dot_tn(attn[:, cols], ours) + dot_tn(
            attn_other[:, cols], g_other[:, pl.ds(start, size)]
        )

    def z_part(i, carry):
        o = i + 1
        to = lax.rem(z + o, nz)
        pz[to] = product(to, split, rest).astype(bf16).reshape(pz.shape[1:])

        @pl.when(o < nz)
        def _():
            z_copy(o).start()

        return carry

    def x_part(i, carry):
        px[i] = product(i, 0, split).astype(bf16).reshape(px.shape[1:])
        return carry

    lax.fori_loop(0, nz, z_part, 0)
    lax.fori_loop(0, nz, x_part, 0)
    pass_quarters()
    pass_halves()
    for copy in done:
        copy.wait()

    def project_back(i, carry):
        o = i + 1
        to = lax.rem(me + o, n)
        cols = block(to, width)
        ga[:, cols] = dot_nt(gv[...], wf[cols, :]).astype(bf16)

        @pl.when(o < n)
        def _():
            for h in range(heads):
                out_copy(3, ga, gh, o, h).start()

        @pl.when(o == n)
        def _():
            for h in range(heads):
                out_own(3, ga, gh, h).start()

        return carry

    lax.fori_loop(0, n, project_back, 0)
    for copy in x_copies:
        copy.start()

    def mix(i, carry):
        cols = block(i, 2 * HEAD)
        mixed[:, cols] = jnp.dot(
            attn[...], wf[:, cols], preferred_element_type=jnp.float32
        ).astype(bf16)
        return carry

    steps = model // (2 * HEAD)
    lax.fori_loop(0, steps // 2, mix, 0)

    def xz_copy(o):
        return send_to(
            x_sum.at[lax.rem(z + o, nz)], xzin.at[o], xzs.at[o], xzr.at[o], line(o), me
        )

    def add_x():
        for copy in x_copies:
            copy.wait()
        for i in range(nz):
            x_sum[i] = (
                wide(px[i, me]) + sum(wide(xin[o, i]) for o in range(1, n))
            ).astype(bf16)
        for o in range(1, nz):
            xz_copy(o).start()

    def backward_head(h, carry):
        for o in range(1, n):
            out_copy(3, ga, gh, o, h).wait()
        out_own(3, ga, gh, h).wait()
        cols = block(h, HEAD)
        dk_sum[...] = jnp.zeros_like(dk_sum)
        dv_sum[...] = jnp.zeros_like(dv_sum)
        for t in range(n):
            here = pl.ds(t * rows, rows)
            query, grad = qh[here, cols], gh[here, cols]
            level = log_total[h, t]
            delta = jnp.sum(
                jnp.transpose(wide(grad) * wide(ah[here, cols])), axis=0, keepdims=True
            )
            out = jnp.zeros((HEAD, rows), jnp.float32)
            for u in window(t, n):
                there = pl.ds(u * rows, rows)
                key, value = kh[there, cols], vh[there, cols]
                weight = jnp.exp(dot_nt(key, query) * SCALE + (tile_bias(near, t, u) - level))
                dscore = (weight * (dot_nt(value, grad) - delta) * SCALE).astype(bf16)
                out += dot_tn(key, dscore)
                dk_sum[there, :] += jnp.dot(dscore, query, preferred_element_type=jnp.float32)
                dv_sum[there, :] += jnp.dot(
                    weight.astype(bf16), grad, preferred_element_type=jnp.float32
                )
            dqh[here, cols] = jnp.transpose(out).astype(bf16)
        give(1, dqh, dq, h)
        dkh[:, cols] = dk_sum[...].astype(bf16)
        give(2, dkh, dk, h)
        dvh[:, cols] = dv_sum[...].astype(bf16)
        give(3, dvh, dv, h)
        pl.when(h == min(1, heads - 1))(add_x)
        return carry

    lax.fori_loop(0, heads, backward_head, 0)
    for o in range(1, nz):
        z_copy(o).wait()
    for i in range(n):
        z_sum[i] = (wide(pz[z, i]) + sum(wide(zin[o, i]) for o in range(1, nz))).astype(bf16)
    zx_copies = [
        send(z_sum.at[column(o)], zxin.at[o], zxs.at[o], zxr.at[o], column(o))
        for o in range(1, n)
    ]
    for copy in zx_copies:
        copy.start()
    lax.fori_loop(steps // 2, steps, mix, 0)
    for o in range(1, nz):
        xz_copy(o).wait()
    for copy in zx_copies:
        copy.wait()
    total[:, pl.ds(0, split)] = (
        wide(x_sum[z]) + sum(wide(xzin[o]) for o in range(1, nz))
    ).astype(bf16)
    total[:, pl.ds(split, rest)] = (
        wide(z_sum[me]) + sum(wide(zxin[o]) for o in range(1, n))
    ).astype(bf16)
    my_part = gw.at[block(lax.rem(me, per), piece), block(core, half)]

    def shares(start):
        for o in range(n):

            def remote():
                copy = send_to(total, my_part, fs.at[o], fr.at[core * n + me], heir, column(o))
                copy.start() if start else copy.wait_send()

            def local():
                copy = pltpu.make_async_copy(total, my_part, f_own)
                copy.start() if start else copy.wait()

            if o > 0:
                remote()
            else:
                pl.when(heir != mine_dp)(remote)
                pl.when(heir == mine_dp)(local)

    shares(True)
    for h in range(heads):
        take(1, dqh, dq, h)
        take(2, dkh, dk, h)
        take(3, dvh, dv, h)
    shares(False)
    for c in range(2):
        for j in range(per):
            source = core * per + j
            part = gw.at[pl.ds(j * piece, piece), pl.ds(c * half, half)]

            @pl.when(jnp.logical_or(source != me, core != c))
            def _():
                send_to(total, part, fs.at[0], fr.at[c * n + source], twin, me).wait_recv()


def sems(*shape):
    return pltpu.SemaphoreType.DMA(shape)


def heads_on_device(n, query, key_in, value_in, out_weight, grad_out, neighbours):
    upstream = grad_out[0]
    rows, model_cols = query.shape[1:]
    width = model_cols // n
    heads = width // HEAD
    bf16, f32 = jnp.bfloat16, jnp.float32
    nz = lax.axis_size("dp") // 2
    depth, out_cols = out_weight.shape
    half = out_cols // 2
    split = half // (3 * HEAD) * HEAD
    piece = model_cols // (nz * n)
    hbm = pl.BlockSpec(memory_space=pl.ANY)
    vmem = pl.BlockSpec(memory_space=pltpu.VMEM)
    smem = pl.BlockSpec(memory_space=pltpu.SMEM)
    wide = jax.ShapeDtypeStruct((rows, model_cols), bf16)
    tall = pltpu.VMEM((n * rows, width), bf16)
    sums = pltpu.VMEM((n * rows, HEAD), f32)
    rest = half - split
    dq, dk, dv, grad_weight, mixed = pl.pallas_call(
        functools.partial(layer_kernel, n, nz),
        out_shape=(
            wide, wide, wide,
            jax.ShapeDtypeStruct((depth, out_cols), bf16),
            jax.ShapeDtypeStruct((rows, out_cols), bf16),
        ),
        in_specs=[smem] + [hbm] * 5,
        out_specs=(hbm, hbm, hbm, hbm, vmem),
        scratch_shapes=[
            pltpu.VMEM((rows, model_cols), bf16),
            pltpu.VMEM((rows, model_cols), bf16),
            pltpu.VMEM((rows, out_cols), bf16),
            pltpu.VMEM((rows, half), bf16),
            pltpu.VMEM((model_cols, out_cols), bf16),
            pltpu.VMEM((rows, model_cols), bf16),
            tall, tall, tall, tall, tall, tall, tall, tall,
            pltpu.VMEM((heads, n, 1, rows), f32),
            sums, sums,
            pltpu.VMEM((nz, n, piece, split), bf16),
            pltpu.VMEM((nz, n, piece, rest), bf16),
            pltpu.VMEM((n, nz, piece, split), bf16),
            pltpu.VMEM((nz, piece, split), bf16),
            pltpu.VMEM((nz, piece, split), bf16),
            pltpu.VMEM((nz, n, piece, rest), bf16),
            pltpu.VMEM((n, piece, rest), bf16),
            pltpu.VMEM((n, piece, rest), bf16),
            pltpu.VMEM((piece, half), bf16),
            sems(4, n, heads), sems(4, n, heads), sems(4, heads),
            sems(4, n, heads), sems(4, n, heads), sems(4, heads), sems(2),
            sems(3), sems(3), sems(nz), sems(nz), sems(nz), sems(nz), sems(nz, n), sems(nz, n),
            sems(nz, n), sems(nz, n), sems(nz), sems(nz),
            sems(n), sems(n), sems(nz), sems(nz), sems(nz), sems(nz), sems(n), sems(n),
            sems(n), sems(2 * n), pltpu.SemaphoreType.DMA,
        ],
        compiler_params=pltpu.CompilerParams(
            collective_id=0, has_side_effects=True, vmem_limit_bytes=60 * 2**20
        ),
        name="layer",
    )(neighbours, query[0], key_in[0], value_in[0], upstream, out_weight)
    grad_weight = grad_weight.astype(f32)
    return (mixed[None], dq[None], dk[None], dv[None], grad_weight)


def solution(mesh):
    n = mesh.shape["space"]

    def on_device(query, *rest):
        if query.shape[2] % (n * HEAD) == 0 and n % 2 == 0 and mesh.shape["dp"] % 2 == 0:
            return heads_on_device(n, query, *rest)
        return halo_on_device(query, *rest)

    return jax.shard_map(
        on_device,
        mesh=mesh,
        in_specs=(
            P("dp", "space", None),
            P("dp", "space", None),
            P("dp", "space", None),
            P("dp", None),
            P("dp", "space", None),
            P(),
        ),
        out_specs=(
            P("dp", "space", None),
            P("dp", "space", None),
            P("dp", "space", None),
            P("dp", "space", None),
            P("dp", None),
        ),
        check_vma=False,
    )
```

```python
import functools
import math

import jax
import jax.numpy as jnp
from jax import lax
from jax.experimental import pallas as pl
from jax.experimental.pallas import tpu as pltpu
from jax.sharding import PartitionSpec as P

HEAD = 128


masked_score = -1e30


def padded(x, sides, width):
    for axis, dim in sides:
        size, length = (lax.axis_size(axis), x.shape[dim])
        up = [(i, (i + 1) % size) for i in range(size - 1)]
        down = [(j, i) for i, j in up]
        last = lax.slice_in_dim(x, length - width, length, axis=dim)
        initial = lax.slice_in_dim(x, 0, width, axis=dim)
        before = lax.ppermute(last, axis, up)
        after = lax.ppermute(initial, axis, down)
        x = jnp.concatenate([before, x, after], axis=dim)
    return x


def halo_on_device(query, key_in, value_in, out_weight, grad_out, neighbours):
    query_rows = query[0]
    key_rows = key_in[0]
    value_rows = value_in[0]
    upstream = grad_out[0]
    tile_rows, model_cols = query_rows.shape
    head_count = model_cols // HEAD
    score_scale = 1.0 / math.sqrt(HEAD)
    tile_total = neighbours.shape[0]
    device_tile = lax.axis_index("space")
    window_tiles = device_tile - 1 + jnp.arange(3, dtype=jnp.int32)
    own_list = neighbours[device_tile]
    key_live = jnp.any(
        (own_list[None, :] == window_tiles[:, None]) & (own_list[None, :] >= 0), axis=1
    )
    inside = (window_tiles >= 0) & (window_tiles < tile_total)
    their_lists = neighbours[jnp.clip(window_tiles, 0, tile_total - 1)]
    query_live = inside & jnp.any(their_lists == device_tile, axis=1)
    key_mask = jnp.repeat(key_live, tile_rows)
    query_mask = jnp.repeat(query_live, tile_rows)
    key_value = jnp.stack([key_rows, value_rows])
    kv_near = padded(key_value, (("space", 1),), tile_rows)
    key_heads = kv_near[0].reshape(3 * tile_rows, head_count, HEAD)
    value_heads = kv_near[1].reshape(3 * tile_rows, head_count, HEAD)
    query_heads = query_rows.reshape(tile_rows, head_count, HEAD)
    scores = (
        jnp.einsum("ihd,jhd->hij", query_heads, key_heads, preferred_element_type=jnp.float32)
        * score_scale
    )
    scores = jnp.where(key_mask[None, None, :], scores, masked_score)
    row_max = jnp.max(scores, axis=2, keepdims=True)
    log_total = (row_max + jnp.log(jnp.sum(jnp.exp(scores - row_max), axis=2, keepdims=True)))[
        ..., 0
    ]
    weights = jnp.exp(scores - log_total[..., None])
    weights_bf = weights.astype(jnp.bfloat16)
    attn = (
        jnp.einsum("hij,jhd->ihd", weights_bf, value_heads, preferred_element_type=jnp.float32)
        .reshape(tile_rows, model_cols)
        .astype(jnp.bfloat16)
    )
    shard_piece = lax.all_gather(out_weight, "dp", axis=0, tiled=True)
    attn_cols = attn
    mixed_sum = jnp.dot(attn_cols, shard_piece, preferred_element_type=jnp.float32)
    new_cols = lax.dot_general(
        upstream, shard_piece, (((1,), (1,)), ((), ())), preferred_element_type=jnp.float32
    )
    back_cols = new_cols
    mixed_sum, back_cols = (mixed_sum, back_cols)
    mixed = mixed_sum.astype(jnp.bfloat16)
    grad_attn = back_cols.astype(jnp.bfloat16)
    grad_heads = grad_attn.reshape(tile_rows, head_count, HEAD)
    deltas = jnp.sum(
        grad_heads.astype(jnp.float32)
        * attn.reshape(tile_rows, head_count, HEAD).astype(jnp.float32),
        axis=2,
    ).T
    dprob = jnp.einsum("ihd,jhd->hij", grad_heads, value_heads, preferred_element_type=jnp.float32)
    dscore = (weights * (dprob - deltas[:, :, None]) * score_scale).astype(jnp.bfloat16)
    grad_query = (
        jnp.einsum("hij,jhd->ihd", dscore, key_heads, preferred_element_type=jnp.float32)
        .reshape(tile_rows, model_cols)
        .astype(jnp.bfloat16)
    )
    stat_pair = jnp.stack([log_total, deltas])
    stat_near = padded(stat_pair, (("space", 2),), tile_rows)
    query_grad = jnp.stack([query_rows, grad_attn])
    query_near = padded(query_grad, (("space", 1),), tile_rows)
    far_queries = query_near[0].reshape(3 * tile_rows, head_count, HEAD)
    far_grads = query_near[1].reshape(3 * tile_rows, head_count, HEAD)
    own_keys = key_rows.reshape(tile_rows, head_count, HEAD)
    own_values = value_rows.reshape(tile_rows, head_count, HEAD)
    back_scores = (
        jnp.einsum("jhd,ihd->hji", far_queries, own_keys, preferred_element_type=jnp.float32)
        * score_scale
    )
    back_weights = jnp.where(
        query_mask[None, :, None], jnp.exp(back_scores - stat_near[0][:, :, None]), 0.0
    )
    back_bf = back_weights.astype(jnp.bfloat16)
    grad_value = (
        jnp.einsum("hji,jhd->ihd", back_bf, far_grads, preferred_element_type=jnp.float32)
        .reshape(tile_rows, model_cols)
        .astype(jnp.bfloat16)
    )
    back_dprob = jnp.einsum(
        "jhd,ihd->hji", far_grads, own_values, preferred_element_type=jnp.float32
    )
    back_dscore = (back_weights * (back_dprob - stat_near[1][:, :, None]) * score_scale).astype(
        jnp.bfloat16
    )
    grad_key = (
        jnp.einsum("hji,jhd->ihd", back_dscore, far_queries, preferred_element_type=jnp.float32)
        .reshape(tile_rows, model_cols)
        .astype(jnp.bfloat16)
    )
    attn_cols = attn
    partial_rows = lax.psum_scatter(
        lax.dot_general(
            attn_cols, upstream, (((0,), (0,)), ((), ())), preferred_element_type=jnp.float32
        ),
        ("dp", "space"),
        scatter_dimension=0,
        tiled=True,
    )
    grad_weight = lax.all_gather(partial_rows, "space", axis=0, tiled=True)
    return (mixed[None], grad_query[None], grad_key[None], grad_value[None], grad_weight)


MESH = pl.DeviceIdType.MESH
SCALE = 1.0 / math.sqrt(HEAD)


def window(tile, tiles):
    return range(max(0, tile - 1), min(tiles, tile + 2))


def tile_bias(near, tile, other):
    live = near[tile, 0] == other
    for slot in range(1, near.shape[1]):
        live = jnp.logical_or(live, near[tile, slot] == other)
    return jnp.where(live, 0.0, masked_score).astype(jnp.float32)


def dot_nt(a, b):
    return lax.dot_general(a, b, (((1,), (1,)), ((), ())), preferred_element_type=jnp.float32)


def dot_tn(a, b):
    return lax.dot_general(a, b, (((0,), (0,)), ((), ())), preferred_element_type=jnp.float32)


def place(nz):
    row = lax.axis_index("dp")
    return row // 2, row % 2, lax.axis_index("space")


def greet(peers):
    barrier = pltpu.get_barrier_semaphore()
    for row, column in peers:
        pl.semaphore_signal(
            barrier, inc=1, device_id={"dp": row, "space": column}, device_id_type=MESH
        )
    pl.semaphore_wait(barrier, len(peers))


def send_to(src, dst, send_sem, recv_sem, row, column):
    return pltpu.make_async_remote_copy(
        src_ref=src,
        dst_ref=dst,
        send_sem=send_sem,
        recv_sem=recv_sem,
        device_id={"dp": row, "space": column},
        device_id_type=MESH,
    )


def send(src, dst, send_sem, recv_sem, peer):
    return send_to(src, dst, send_sem, recv_sem, lax.axis_index("dp"), peer)


def block(index, size):
    return pl.ds(pl.multiple_of(index * size, size), size)


def layer_kernel(
    n, nz, near, q, k, v, g, w, dq, dk, dv, gw, mixed,
    attn, attn_other, gv, g_other, wf, ga, qh, kh, vh, ah, gh, dqh, dkh, dvh,
    log_total, dk_sum, dv_sum, px, pz, xin, x_sum, xzin, zin, z_sum, zxin, total,
    send_sem, recv_sem, own_sem, back_send, back_recv, back_own, load_sem,
    core_send, core_recv, zq_send, zq_recv, zh_send, zh_recv, sq_send, sq_recv,
    cq_send, cq_recv, ch_send, ch_recv,
    xs, xr, xzs, xzr, zs, zr, zxs, zxr, fs, fr, f_own,
):
    z, core, me = place(nz)
    mine_dp = 2 * z + core
    twin = 2 * z + 1 - core
    rows = q.shape[0]
    width = qh.shape[1]
    heads = width // HEAD
    depth, model = w.shape
    half = model // 2
    quarter = half // n
    split = px.shape[3]
    rest = pz.shape[3]
    piece = px.shape[2]
    per = n // 2
    heir = 2 * z + me // per
    upper = pl.ds(half, half)
    shard = block(mine_dp, depth)
    my_quarter = block(me, quarter)
    mine = block(me, rows)
    bf16 = jnp.bfloat16

    def column(o):
        return lax.rem(me + o, n)

    def line(o):
        return 2 * lax.rem(z + o, nz) + core

    def wide(ref):
        return ref.astype(jnp.float32)

    greet(
        [(mine_dp, column(o)) for o in range(1, n)]
        + [(line(o), me) for o in range(1, nz)]
        + [(twin, column(o)) for o in range(n)]
    )
    done = []

    def begin(copy):
        copy.start()
        done.append(copy)

    def out_copy(a, src, dst, o, h):
        peer = column(o)
        return send(
            src.at[:, block(peer * heads + h, HEAD)], dst.at[mine, block(h, HEAD)],
            send_sem.at[a, o, h], recv_sem.at[a, o, h], peer,
        )

    def out_own(a, src, dst, h):
        return pltpu.make_async_copy(
            src.at[:, block(me * heads + h, HEAD)], dst.at[mine, block(h, HEAD)], own_sem.at[a, h]
        )

    def back_copy(a, src, dst, o, h):
        peer = column(o)
        return send(
            src.at[block(peer, rows), block(h, HEAD)], dst.at[:, block(me * heads + h, HEAD)],
            back_send.at[a, o, h], back_recv.at[a, o, h], peer,
        )

    def back_local(a, src, dst, h):
        return pltpu.make_async_copy(
            src.at[mine, block(h, HEAD)], dst.at[:, block(me * heads + h, HEAD)], back_own.at[a, h]
        )

    def give(a, src, dst, h):
        for o in range(1, n):
            back_copy(a, src, dst, o, h).start()
        back_local(a, src, dst, h).start()

    def take(a, src, dst, h):
        for o in range(1, n):
            back_copy(a, src, dst, o, h).wait()
        back_local(a, src, dst, h).wait()

    inputs = ((q, qh), (k, kh), (v, vh))

    def start_head(h, carry):
        for a, (src, dst) in enumerate(inputs):
            for o in range(1, n):
                out_copy(a, src, dst, o, h).start()
            out_own(a, src, dst, h).start()
        return carry

    lax.fori_loop(0, 1, start_head, 0)
    from_z, halves, quarters = [], [], []
    for o in range(1, nz):
        copy = send_to(
            w.at[:, my_quarter], wf.at[shard, my_quarter], zq_send.at[o], zq_recv.at[o],
            line(o), me,
        )
        copy.start()
        from_z.append(copy)
    lax.fori_loop(1, heads, start_head, 0)
    for o in range(1, nz):
        copy = send_to(
            w.at[:, upper], wf.at[shard, upper], zh_send.at[o], zh_recv.at[o], line(o), me
        )
        copy.start()
        halves.append(copy)
    load_g = pltpu.make_async_copy(g, gv, load_sem.at[0])
    load_g.start()
    begin(pltpu.make_async_copy(w, wf.at[shard], load_sem.at[1]))
    begin(send_to(w, wf.at[shard], core_send.at[0], core_recv.at[0], twin, me))
    other_g = send_to(
        g.at[:, block(1 - core, half)], g_other, core_send.at[1], core_recv.at[1], twin, me
    )
    other_g.start()

    def theirs(o):
        return block(line(nz - o), depth)

    def pass_from_z():
        for o in range(1, nz):
            from_z[o - 1].wait()
            part = wf.at[theirs(o), my_quarter]
            for p in range(1, n):
                send(part, part, sq_send.at[o, p], sq_recv.at[o, p], column(p)).start()
            send_to(part, part, cq_send.at[o, 0], cq_recv.at[o, 0], twin, me).start()

    def pass_quarters():
        for o in range(1, nz):
            part = wf.at[theirs(o), my_quarter]
            for p in range(1, n):
                send(part, part, sq_send.at[o, p], sq_recv.at[o, p], column(p)).wait()
                came = wf.at[theirs(o), block(column(n - p), quarter)]
                begin(send_to(came, came, cq_send.at[o, p], cq_recv.at[o, p], twin, me))
            done.append(send_to(part, part, cq_send.at[o, 0], cq_recv.at[o, 0], twin, me))

    def pass_halves():
        for o in range(1, nz):
            halves[o - 1].wait()
            part = wf.at[theirs(o), upper]
            begin(send_to(part, part, ch_send.at[o], ch_recv.at[o], twin, me))

    def forward_head(h, carry):
        for a, (src, dst) in enumerate(inputs):
            for o in range(1, n):
                out_copy(a, src, dst, o, h).wait()
            out_own(a, src, dst, h).wait()
        cols = block(h, HEAD)
        for t in range(n):
            here = pl.ds(t * rows, rows)
            query = qh[here, cols]
            scores = [
                dot_nt(query, kh[pl.ds(u * rows, rows), cols]) * SCALE + tile_bias(near, t, u)
                for u in window(t, n)
            ]
            top = functools.reduce(
                jnp.maximum, [jnp.max(s, axis=1, keepdims=True) for s in scores]
            )
            parts = [jnp.exp(s - top) for s in scores]
            summed = sum(jnp.sum(p, axis=1, keepdims=True) for p in parts)
            out = sum(
                jnp.dot(
                    p.astype(bf16),
                    vh[pl.ds(u * rows, rows), cols],
                    preferred_element_type=jnp.float32,
                )
                for u, p in zip(window(t, n), parts)
            )
            ah[here, cols] = (out / summed).astype(bf16)
            level = jnp.broadcast_to(top + jnp.log(summed), (rows, HEAD))
            log_total[h, t] = jnp.transpose(level)[0:1, :]
        give(0, ah, attn, h)
        pl.when(h == 0)(pass_from_z)
        return carry

    lax.fori_loop(0, heads, forward_head, 0)
    for h in range(heads):
        take(0, ah, attn, h)
    other_attn = send_to(attn, attn_other, core_send.at[2], core_recv.at[2], twin, me)
    other_attn.start()
    load_g.wait()
    other_g.wait()
    other_attn.wait()

    def z_copy(o):
        return send_to(
            pz.at[lax.rem(z + o, nz)], zin.at[o], zs.at[o], zr.at[o], line(o), me
        )

    x_copies = [
        send(px.at[:, column(o)], xin.at[o], xs.at[o], xr.at[o], column(o)) for o in range(1, n)
    ]

    def product(i, start, size):
        cols = block(i, n * piece)
        ours = gv[:, pl.ds(pl.multiple_of(core * half + start, HEAD), size)]
        return dot_tn(attn[:, cols], ours) + dot_tn(
            attn_other[:, cols], g_other[:, pl.ds(start, size)]
        )

    def z_part(i, carry):
        o = i + 1
        to = lax.rem(z + o, nz)
        pz[to] = product(to, split, rest).astype(bf16).reshape(pz.shape[1:])

        @pl.when(o < nz)
        def _():
            z_copy(o).start()

        return carry

    def x_part(i, carry):
        px[i] = product(i, 0, split).astype(bf16).reshape(px.shape[1:])
        return carry

    lax.fori_loop(0, nz, z_part, 0)
    pass_quarters()
    lax.fori_loop(0, nz, x_part, 0)
    for copy in x_copies:
        copy.start()
    pass_halves()
    for copy in done:
        copy.wait()

    def project_back(i, carry):
        o = i + 1
        to = lax.rem(me + o, n)
        cols = block(to, width)
        ga[:, cols] = dot_nt(gv[...], wf[cols, :]).astype(bf16)

        @pl.when(o < n)
        def _():
            for h in range(heads):
                out_copy(3, ga, gh, o, h).start()

        @pl.when(o == n)
        def _():
            for h in range(heads):
                out_own(3, ga, gh, h).start()

        return carry

    lax.fori_loop(0, n, project_back, 0)

    def mix(i, carry):
        cols = block(i, 2 * HEAD)
        mixed[:, cols] = jnp.dot(
            attn[...], wf[:, cols], preferred_element_type=jnp.float32
        ).astype(bf16)
        return carry

    steps = model // (2 * HEAD)
    lax.fori_loop(0, steps // 2, mix, 0)

    def xz_copy(o):
        return send_to(
            x_sum.at[lax.rem(z + o, nz)], xzin.at[o], xzs.at[o], xzr.at[o], line(o), me
        )

    def add_x():
        for copy in x_copies:
            copy.wait()
        for i in range(nz):
            x_sum[i] = (
                wide(px[i, me]) + sum(wide(xin[o, i]) for o in range(1, n))
            ).astype(bf16)
        for o in range(1, nz):
            xz_copy(o).start()

    def backward_head(h, carry):
        for o in range(1, n):
            out_copy(3, ga, gh, o, h).wait()
        out_own(3, ga, gh, h).wait()
        cols = block(h, HEAD)
        dk_sum[...] = jnp.zeros_like(dk_sum)
        dv_sum[...] = jnp.zeros_like(dv_sum)
        for t in range(n):
            here = pl.ds(t * rows, rows)
            query, grad = qh[here, cols], gh[here, cols]
            level = log_total[h, t]
            delta = jnp.sum(
                jnp.transpose(wide(grad) * wide(ah[here, cols])), axis=0, keepdims=True
            )
            out = jnp.zeros((rows, HEAD), jnp.float32)
            for u in window(t, n):
                there = pl.ds(u * rows, rows)
                key, value = kh[there, cols], vh[there, cols]
                weight = jnp.exp(dot_nt(key, query) * SCALE + (tile_bias(near, t, u) - level))
                dscore = (weight * (dot_nt(value, grad) - delta) * SCALE).astype(bf16)
                out += dot_tn(dscore, key)
                dk_sum[there, :] += jnp.dot(dscore, query, preferred_element_type=jnp.float32)
                dv_sum[there, :] += jnp.dot(
                    weight.astype(bf16), grad, preferred_element_type=jnp.float32
                )
            dqh[here, cols] = out.astype(bf16)
        give(1, dqh, dq, h)
        dkh[:, cols] = dk_sum[...].astype(bf16)
        give(2, dkh, dk, h)
        dvh[:, cols] = dv_sum[...].astype(bf16)
        give(3, dvh, dv, h)
        pl.when(h == 0)(add_x)
        return carry

    lax.fori_loop(0, heads, backward_head, 0)
    for o in range(1, nz):
        z_copy(o).wait()
    for i in range(n):
        z_sum[i] = (wide(pz[z, i]) + sum(wide(zin[o, i]) for o in range(1, nz))).astype(bf16)
    zx_copies = [
        send(z_sum.at[column(o)], zxin.at[o], zxs.at[o], zxr.at[o], column(o))
        for o in range(1, n)
    ]
    for copy in zx_copies:
        copy.start()
    lax.fori_loop(steps // 2, steps, mix, 0)
    for o in range(1, nz):
        xz_copy(o).wait()
    for copy in zx_copies:
        copy.wait()
    total[:, pl.ds(0, split)] = (
        wide(x_sum[z]) + sum(wide(xzin[o]) for o in range(1, nz))
    ).astype(bf16)
    total[:, pl.ds(split, rest)] = (
        wide(z_sum[me]) + sum(wide(zxin[o]) for o in range(1, n))
    ).astype(bf16)
    my_part = gw.at[block(lax.rem(me, per), piece), block(core, half)]

    def shares(start):
        for o in range(n):

            def remote():
                copy = send_to(total, my_part, fs.at[o], fr.at[core * n + me], heir, column(o))
                copy.start() if start else copy.wait_send()

            def local():
                copy = pltpu.make_async_copy(total, my_part, f_own)
                copy.start() if start else copy.wait()

            if o > 0:
                remote()
            else:
                pl.when(heir != mine_dp)(remote)
                pl.when(heir == mine_dp)(local)

    shares(True)
    for h in range(heads):
        take(1, dqh, dq, h)
        take(2, dkh, dk, h)
        take(3, dvh, dv, h)
    shares(False)
    for c in range(2):
        for j in range(per):
            source = core * per + j
            part = gw.at[pl.ds(j * piece, piece), pl.ds(c * half, half)]

            @pl.when(jnp.logical_or(source != me, core != c))
            def _():
                send_to(total, part, fs.at[0], fr.at[c * n + source], twin, me).wait_recv()


def sems(*shape):
    return pltpu.SemaphoreType.DMA(shape)


def heads_on_device(n, query, key_in, value_in, out_weight, grad_out, neighbours):
    upstream = grad_out[0]
    rows, model_cols = query.shape[1:]
    width = model_cols // n
    heads = width // HEAD
    bf16, f32 = jnp.bfloat16, jnp.float32
    nz = lax.axis_size("dp") // 2
    depth, out_cols = out_weight.shape
    half = out_cols // 2
    split = half // (3 * HEAD) * HEAD
    piece = model_cols // (nz * n)
    hbm = pl.BlockSpec(memory_space=pl.ANY)
    vmem = pl.BlockSpec(memory_space=pltpu.VMEM)
    smem = pl.BlockSpec(memory_space=pltpu.SMEM)
    wide = jax.ShapeDtypeStruct((rows, model_cols), bf16)
    tall = pltpu.VMEM((n * rows, width), bf16)
    sums = pltpu.VMEM((n * rows, HEAD), f32)
    rest = half - split
    dq, dk, dv, grad_weight, mixed = pl.pallas_call(
        functools.partial(layer_kernel, n, nz),
        out_shape=(
            wide, wide, wide,
            jax.ShapeDtypeStruct((depth, out_cols), bf16),
            jax.ShapeDtypeStruct((rows, out_cols), bf16),
        ),
        in_specs=[smem] + [hbm] * 5,
        out_specs=(hbm, hbm, hbm, hbm, vmem),
        scratch_shapes=[
            pltpu.VMEM((rows, model_cols), bf16),
            pltpu.VMEM((rows, model_cols), bf16),
            pltpu.VMEM((rows, out_cols), bf16),
            pltpu.VMEM((rows, half), bf16),
            pltpu.VMEM((model_cols, out_cols), bf16),
            pltpu.VMEM((rows, model_cols), bf16),
            tall, tall, tall, tall, tall, tall, tall, tall,
            pltpu.VMEM((heads, n, 1, rows), f32),
            sums, sums,
            pltpu.VMEM((nz, n, piece, split), bf16),
            pltpu.VMEM((nz, n, piece, rest), bf16),
            pltpu.VMEM((n, nz, piece, split), bf16),
            pltpu.VMEM((nz, piece, split), bf16),
            pltpu.VMEM((nz, piece, split), bf16),
            pltpu.VMEM((nz, n, piece, rest), bf16),
            pltpu.VMEM((n, piece, rest), bf16),
            pltpu.VMEM((n, piece, rest), bf16),
            pltpu.VMEM((piece, half), bf16),
            sems(4, n, heads), sems(4, n, heads), sems(4, heads),
            sems(4, n, heads), sems(4, n, heads), sems(4, heads), sems(2),
            sems(3), sems(3), sems(nz), sems(nz), sems(nz), sems(nz), sems(nz, n), sems(nz, n),
            sems(nz, n), sems(nz, n), sems(nz), sems(nz),
            sems(n), sems(n), sems(nz), sems(nz), sems(nz), sems(nz), sems(n), sems(n),
            sems(n), sems(2 * n), pltpu.SemaphoreType.DMA,
        ],
        compiler_params=pltpu.CompilerParams(
            collective_id=0, has_side_effects=True, vmem_limit_bytes=60 * 2**20
        ),
        name="layer",
    )(neighbours, query[0], key_in[0], value_in[0], upstream, out_weight)
    grad_weight = grad_weight.astype(f32)
    return (mixed[None], dq[None], dk[None], dv[None], grad_weight)


def solution(mesh):
    n = mesh.shape["space"]

    def on_device(query, *rest):
        if query.shape[2] % (n * HEAD) == 0 and n % 2 == 0 and mesh.shape["dp"] % 2 == 0:
            return heads_on_device(n, query, *rest)
        return halo_on_device(query, *rest)

    return jax.shard_map(
        on_device,
        mesh=mesh,
        in_specs=(
            P("dp", "space", None),
            P("dp", "space", None),
            P("dp", "space", None),
            P("dp", None),
            P("dp", "space", None),
            P(),
        ),
        out_specs=(
            P("dp", "space", None),
            P("dp", "space", None),
            P("dp", "space", None),
            P("dp", "space", None),
            P("dp", None),
        ),
        check_vma=False,
    )
```
